32 devices in a mesh: enc: 4 (over z), llm: 2 (over x), tp: 4 (over y, core).
Axes of the slice: x: 2, y: 2, z: 4, core: 2. Of those that a mesh axis runs over, the one named last changes fastest.
Arguments:
- visual: bfloat16 [4, 2, 4, 4, 8192], P('enc', 'llm'), may hold values from -6 to 6
- counts: int32 [4, 2, 4], P('enc', 'llm'), may hold values from 0 to 4, as said below
- merger_bias: float32 [8192], replicated, may hold values from -3 to 3
- norm_gain: float32 [8192], replicated, may hold values from 0.1 to 1.9
- kv_weight: bfloat16 [8192, 2048], P(None, 'tp'), may hold values from -0.0625 to 0.0625
- kv_cotangent: bfloat16 [4, 2, 4, 4, 2048], P('enc', 'llm', None, None, 'tp'), may hold values from -6 to 6
Outputs:
- key_values: bfloat16 [4, 2, 4, 4, 2048], P('enc', 'llm', None, None, 'tp')
- visual_grad: bfloat16 [4, 2, 4, 4, 8192], P('enc', 'llm', None, None, 'tp')
- bias_grad: float32 [8192], P('tp')
The draws below stay inside these ranges and needn't reach their ends.
Inputs may be any that keep to these rules, and one draw needn't show every extreme that they name: Slots c < counts[s, g, b] of block (s, g, b) hold live merged patch blocks, the others hold unused data. For every group g some bucket b receives 4 live slots from every source s.
All inputs are finite; a program needn't handle non-finite values.
Results may differ from the reference program's by a relative error of at most 0.0049.
Values may be sent and summed in bfloat16 or wider, within the bound.
No kernel may reach another device: no remote copies, remote signals or barrier semaphores. Data moves between devices by JAX's collectives and lax.ppermute only.
A program may use at most 64 MiB of HBM per device.

```python
import jax
import jax.numpy as jnp
from jax import lax

D = 8192
CAP = 4
KVD = 2048
N_ENC = 4
N_LLM = 2


def draw_counts(key, part):
    first_key, second_key = jax.random.split(jax.random.fold_in(key, 7))
    base = jax.random.randint(first_key, (N_ENC, N_LLM, N_ENC), 0, CAP + 1)
    full_bucket = jax.random.randint(second_key, (N_LLM,), 0, N_ENC)
    chosen = jnp.arange(N_ENC)[None, :] == full_bucket[:, None]
    return jnp.where(chosen[None, :, :], CAP, base).astype(jnp.int32)


def levels(stream_key, shape, cuts, least, top_value):
    gain, own = 1.0, jax.random.fold_in(stream_key, 6)
    for dim, blocks in cuts:
        steps = jnp.exp(jax.random.uniform(jax.random.fold_in(own, dim), (blocks,), jnp.float32, least / len(cuts), top_value / len(cuts)))
        gain = gain * jnp.repeat(steps, shape[dim] // blocks).reshape([-1 if axis == dim else 1 for axis in range(len(shape))])
    return gain


def scatter_about(rng, dims, scale, reach, cuts=(), kind=jnp.bfloat16):
    entries = jax.random.normal(rng, dims, jnp.float32) * scale
    if len(cuts) > 0:
        entries = levels(rng, dims, cuts, -0.22, 0.18) * entries
    return jnp.clip(entries, min=-reach, max=reach).astype(kind)


def setup_inputs(seed: int = 0) -> dict:
    key_of = jax.random.split(jax.random.key(seed), 7)
    visual = scatter_about(key_of[0], (N_ENC, N_LLM, N_ENC, CAP, D), 1.0, 6.0, ((0, 4), (1, 2)))
    counts = draw_counts(jax.random.fold_in(key_of[6], 71), 0)
    merger_bias = scatter_about(key_of[2], (D,), 0.5, 3.0, (), jnp.float32)
    norm_gain = jnp.clip(1.0 + 0.18 * jax.random.normal(key_of[3], (D,), jnp.float32), 0.1, 1.9)
    kv_weight = scatter_about(key_of[4], (D, KVD), D ** -0.5, 0.0625, ((1, 4),))
    kv_cotangent = scatter_about(key_of[5], (N_ENC, N_LLM, N_ENC, CAP, KVD), 1.0, 6.0, ((0, 4), (1, 2), (4, 4)))
    return dict(visual=visual, counts=counts, merger_bias=merger_bias, norm_gain=norm_gain, kv_weight=kv_weight, kv_cotangent=kv_cotangent)


def reference(visual, counts, merger_bias, norm_gain, kv_weight, kv_cotangent):
    features = visual.shape[4]
    columns = kv_weight.shape[1]
    bucketed = jnp.transpose(visual, (2, 1, 0, 3, 4))
    bucket_counts = jnp.transpose(counts, (2, 1, 0))

    def per_bucket(pieces):
        slot_rows, slot_counts, cot_rows = pieces
        live = lax.broadcasted_iota(jnp.int32, cot_rows.shape[:3], 2) < slot_counts[:, :, None]
        inputs = slot_rows.astype(jnp.float32) + merger_bias
        inv_rms = lax.rsqrt(lax.optimization_barrier(jnp.mean(inputs * inputs, axis=-1, keepdims=True)) + 1e-06)
        normed = (inputs * inv_rms * norm_gain).astype(jnp.bfloat16)
        projected = jnp.dot(normed.reshape(-1, features), kv_weight, preferred_element_type=jnp.float32).reshape(cot_rows.shape)
        live_cols = live[..., None]
        key_out = jnp.where(live_cols, projected, jnp.zeros_like(projected)).astype(jnp.bfloat16)
        masked = jnp.where(live_cols, cot_rows, jnp.zeros_like(cot_rows))
        row_dot = lax.optimization_barrier(jnp.sum(masked.astype(jnp.float32) * projected, axis=-1, keepdims=True))
        grad_normed = lax.dot_general(masked.reshape(-1, columns), kv_weight, (((1,), (1,)), ((), ())), preferred_element_type=jnp.float32).reshape(inputs.shape)
        grad_rows = inv_rms * norm_gain * grad_normed - inputs * (inv_rms * inv_rms) * row_dot / features
        return (key_out, grad_rows.astype(jnp.bfloat16), lax.optimization_barrier(jnp.sum(grad_rows, axis=(0, 1, 2))))
    key_values, grad_bucketed, bias_parts = lax.map(per_bucket, (bucketed, bucket_counts, kv_cotangent))
    visual_grad = jnp.transpose(grad_bucketed, (2, 1, 0, 3, 4))
    return (key_values, visual_grad, lax.optimization_barrier(jnp.sum(bias_parts, axis=0)))
```

```python
import jax
import jax.numpy as jnp
from jax import lax
from jax.sharding import PartitionSpec as P


def is_power(n):
    return n & (n - 1) == 0


def xor_order(blocks, index):
    n = blocks.shape[0]
    bit = 1
    while bit < n:
        pairs = blocks.reshape((n // (2 * bit), 2, bit) + blocks.shape[1:])
        flipped = jnp.flip(pairs, axis=1).reshape(blocks.shape)
        blocks = jnp.where((index & bit) != 0, flipped, blocks)
        bit *= 2
    return blocks


def swap(x, axis, k):
    n = lax.axis_size(axis)
    return lax.ppermute(x, axis, [(i, i ^ k) for i in range(n)])


def exchange(blocks, axis):
    n = lax.axis_size(axis)
    if not is_power(n) or n > 8:
        return lax.all_to_all(blocks, axis, split_axis=0, concat_axis=0, tiled=True)
    index = lax.axis_index(axis)
    ordered = xor_order(blocks, index)
    got = [ordered[0]] + [swap(ordered[k], axis, k) for k in range(1, n)]
    return xor_order(jnp.stack(got), index)


def all_sum(x, axis):
    n = lax.axis_size(axis)
    if not is_power(n) or n > 8:
        return lax.psum(x, axis)
    return x + sum(swap(x, axis, k) for k in range(1, n))


def per_device(visual, counts, merger_bias, norm_gain, kv_weight, kv_cotangent):
    buckets, capacity, features = visual.shape[2:]
    tp_count = lax.axis_size("tp")
    own_width = features // tp_count
    tp_index = lax.axis_index("tp")
    own_start = tp_index * own_width
    columns = kv_weight.shape[1]
    rows = buckets * capacity
    cot_rows = exchange(kv_cotangent[0, 0], "enc").reshape(rows, columns)
    validity = (
        lax.broadcasted_iota(jnp.int32, (buckets, capacity), 1) < counts[0, 0][:, None]
    ).reshape(rows, 1)
    inputs = visual.reshape(rows, features).astype(jnp.float32) + merger_bias
    inv_rms = lax.rsqrt(jnp.mean(inputs * inputs, axis=1, keepdims=True) + 1e-06)
    normed = (inputs * inv_rms * norm_gain).astype(jnp.bfloat16)
    projected = jnp.dot(normed, kv_weight, preferred_element_type=jnp.float32)
    masked_out = jnp.where(validity, projected, jnp.zeros_like(projected)).astype(jnp.bfloat16)
    key_out = exchange(masked_out.reshape(buckets, capacity, columns), "enc")
    masked = jnp.where(validity, cot_rows, jnp.zeros_like(cot_rows))
    part_dots = jnp.sum(masked.astype(jnp.float32) * projected, axis=1)
    grad_part = lax.dot_general(
        masked, kv_weight, (((1,), (1,)), ((), ())), preferred_element_type=jnp.float32
    )
    row_dot = all_sum(part_dots, "tp")[:, None]
    parts = grad_part.reshape(rows, tp_count, own_width).transpose(1, 0, 2)
    ordered = xor_order(parts, tp_index)
    grad_normed = ordered[0]
    for k in range(1, tp_count):
        got = swap(ordered[k].astype(jnp.bfloat16), "tp", k)
        grad_normed = grad_normed + got.astype(jnp.float32)
    own_inputs = lax.dynamic_slice_in_dim(inputs, own_start, own_width, 1)
    own_gain = lax.dynamic_slice_in_dim(norm_gain, own_start, own_width, 0)
    grad_rows = (
        inv_rms * own_gain * grad_normed - own_inputs * (inv_rms * inv_rms) * row_dot / features
    )
    bias_grad = all_sum(all_sum(jnp.sum(grad_rows, axis=0), "enc"), "llm")
    visual_grad = grad_rows.astype(jnp.bfloat16).reshape(1, 1, buckets, capacity, own_width)
    key_values = key_out.reshape(1, 1, buckets, capacity, columns)
    return (key_values, visual_grad, bias_grad)


def solution(mesh):
    return jax.shard_map(
        per_device,
        mesh=mesh,
        in_specs=(
            P("enc", "llm", None, None, None),
            P("enc", "llm", None),
            P(),
            P(),
            P(None, "tp"),
            P("enc", "llm", None, None, "tp"),
        ),
        out_specs=(P("enc", "llm", None, None, "tp"), P("enc", "llm", None, None, "tp"), P("tp")),
        check_vma=False,
    )
```

```python
import functools

import jax
import jax.numpy as jnp
from jax import lax
from jax.experimental import pallas as pl
from jax.experimental.pallas import tpu as pltpu
from jax.sharding import PartitionSpec as P

LANES = 128
PIECES = 3
VMEM = pl.BlockSpec(memory_space=pltpu.VMEM)
SMEM = pl.BlockSpec(memory_space=pltpu.SMEM)
F32 = jnp.float32
BF16 = jnp.bfloat16


def partner(index, k, n):
    if n & (n - 1) == 0:
        return index ^ k, index ^ k
    return lax.rem(index + k, n), lax.rem(index + n - k, n)


def swap(x, axis, k):
    n = lax.axis_size(axis)
    return lax.ppermute(x, axis, [(i, int(partner(i, k, n)[0])) for i in range(n)])


def call(kernel, outs, args, scratch=(), smem=()):
    size = sum(a.size * a.dtype.itemsize for a in (*args, *outs))
    size += sum(4 * functools.reduce(lambda x, y: x * y, s) for s in scratch)
    return pl.pallas_call(
        kernel,
        out_shape=tuple(outs),
        in_specs=[SMEM if i in smem else VMEM for i in range(len(args))],
        out_specs=tuple(VMEM for _ in outs),
        scratch_shapes=[pltpu.VMEM(s, F32) for s in scratch],
        compiler_params=pltpu.CompilerParams(vmem_limit_bytes=int(1.25 * size) + 4 * 2**20),
    )(*args)


def norm_kernel(vis_ref, bias_ref, gain_ref, normed_ref, inv_ref, rows_ref):
    buckets, capacity, features = vis_ref.shape
    for q in range(buckets):
        rows_ref[q * capacity : (q + 1) * capacity, :] = vis_ref[q].astype(F32) + bias_ref[...]
    inputs = rows_ref[...]
    mean = jnp.sum(inputs * inputs, axis=1, keepdims=True) / features
    inv_rms = lax.rsqrt(mean + 1e-06)
    normed_ref[...] = (inputs * inv_rms * gain_ref[...]).astype(BF16)
    inv_ref[...] = jnp.broadcast_to(inv_rms, inv_ref.shape)


def project_kernel(normed_ref, weight_ref, projected_ref):
    projected_ref[...] = jnp.dot(normed_ref[...], weight_ref[...], preferred_element_type=F32)


def backward_kernel(enc, tp, *refs):
    counts_ref, projected_ref, weight_ref = refs[:3]
    cots, refs = refs[3 : 3 + enc], refs[3 + enc :]
    kv_ref, dots_ref, own_ref = refs[:3]
    sends, (picked_ref, masked_ref) = refs[3 : 2 + tp], refs[2 + tp :]
    buckets, capacity, columns = kv_ref.shape
    me, place = lax.axis_index("enc"), lax.axis_index("tp")
    for k in range(enc):
        picked_ref[partner(me, k, enc)[1]] = cots[k][me].astype(F32)
    slot = lax.broadcasted_iota(jnp.int32, (capacity, columns), 0)
    for q in range(buckets):
        rows = slice(q * capacity, (q + 1) * capacity)
        live = slot < counts_ref[0, q]
        masked_ref[rows, :] = jnp.where(live, picked_ref[q], 0.0)
        kv_ref[q] = jnp.where(live, projected_ref[rows, :], 0.0)
    masked = masked_ref[...]
    dots = jnp.sum(masked * projected_ref[...], axis=1, keepdims=True)
    dots = jnp.broadcast_to(dots, dots_ref.shape)
    dots_ref[...] = dots
    lane = lax.broadcasted_iota(jnp.int32, dots.shape, 1)
    pieces, rest = jnp.zeros(dots.shape, F32), dots
    for i in range(PIECES):
        piece = rest.astype(BF16).astype(F32)
        pieces = jnp.where(lane == i, piece, pieces)
        rest = rest - piece
    lhs = masked.astype(BF16)
    width = own_ref.shape[1]
    for k in [*range(1, tp), 0]:
        start = pl.multiple_of(partner(place, k, tp)[0] * width, width)
        part = lax.dot_general(
            lhs,
            weight_ref[pl.ds(start, width), :],
            (((1,), (1,)), ((), ())),
            preferred_element_type=F32,
        )
        if k:
            sends[k - 1][:, :width] = part.astype(BF16)
            sends[k - 1][:, width:] = pieces.astype(BF16)
        else:
            own_ref[...] = part


def combine_kernel(enc, tp, *refs):
    vis_ref, bias_ref, gain_ref, inv_ref, kv_ref, dots_ref, own_ref = refs[:7]
    gots, refs = refs[7 : 6 + tp], refs[6 + tp :]
    grad_ref, total_ref = refs[:2]
    sends, (rows_ref,) = refs[2 : 1 + enc], refs[1 + enc :]
    buckets, capacity, features = vis_ref.shape
    width = own_ref.shape[1]
    me, place = lax.axis_index("enc"), lax.axis_index("tp")
    own = pl.ds(pl.multiple_of(place * width, width), width)
    for q in range(buckets):
        rows_ref[q * capacity : (q + 1) * capacity, :] = (
            vis_ref[q, :, own].astype(F32) + bias_ref[:, own]
        )
    grad_normed, row_dot = own_ref[...], dots_ref[:, :1]
    for got in gots:
        grad_normed = grad_normed + got[:, :width].astype(F32)
        row_dot = row_dot + jnp.sum(got[:, width:].astype(F32), axis=1, keepdims=True)
    inv_rms = inv_ref[:, :1]
    grad_rows = (
        inv_rms * gain_ref[:, own] * grad_normed
        - rows_ref[...] * (inv_rms * inv_rms) * row_dot / features
    )
    grad_ref[...] = grad_rows
    total = jnp.sum(grad_rows, axis=0, keepdims=True)
    chunks = width // LANES
    for j in range(chunks):
        total_ref[j : j + 1, :] = total[:, j * LANES : (j + 1) * LANES]
    for k in range(1, enc):
        sends[k - 1][:chunks, :] = total_ref[...]
        block = kv_ref[partner(me, k, enc)[0]]
        for j in range(block.shape[1] // LANES):
            at = chunks + j * capacity
            sends[k - 1][at : at + capacity, :] = block[:, j * LANES : (j + 1) * LANES]


def round_kernel(grad_ref, out_ref):
    buckets, capacity, _ = out_ref.shape
    for q in range(buckets):
        out_ref[q] = grad_ref[q * capacity : (q + 1) * capacity, :].astype(BF16)


def sum_kernel(chunks, *refs):
    total = refs[0][...]
    for got in refs[1:-1]:
        total = total + got[:chunks, :]
    refs[-1][...] = total


def keys_kernel(enc, kv_ref, *refs):
    gots, out_ref = refs[: enc - 1], refs[enc - 1]
    buckets, capacity, columns = kv_ref.shape
    me = lax.axis_index("enc")
    out_ref[me] = kv_ref[me].astype(BF16)
    chunks = gots[0].shape[0] - capacity * columns // LANES
    for k in range(1, enc):
        source = partner(me, k, enc)[1]
        for j in range(columns // LANES):
            at = chunks + j * capacity
            out_ref[source, :, j * LANES : (j + 1) * LANES] = gots[k - 1][
                at : at + capacity, :
            ].astype(BF16)


def per_device(visual, counts, merger_bias, norm_gain, kv_weight, kv_cotangent):
    buckets, capacity, features = visual.shape[2:]
    enc, llm, tp = (lax.axis_size(a) for a in ("enc", "llm", "tp"))
    width, columns, rows = features // tp, kv_weight.shape[1], buckets * capacity
    chunks = width // LANES
    vis, bias, gain = visual[0, 0], merger_bias[None], norm_gain[None]
    own_cot = kv_cotangent[0, 0]
    struct = jax.ShapeDtypeStruct

    cots = [own_cot] + [swap(own_cot, "enc", k) for k in range(1, enc)]
    normed, inv_rms = call(
        norm_kernel,
        (struct((rows, features), BF16), struct((rows, LANES), F32)),
        (vis, bias, gain),
        scratch=[(rows, features)],
    )
    (projected,) = call(project_kernel, (struct((rows, columns), F32),), (normed, kv_weight))
    kv, dots, own, *sends = call(
        functools.partial(backward_kernel, enc, tp),
        (
            struct((buckets, capacity, columns), F32),
            struct((rows, LANES), F32),
            struct((rows, width), F32),
            *[struct((rows, width + LANES), BF16)] * (tp - 1),
        ),
        (counts[0], projected, kv_weight, *cots),
        scratch=[(buckets, capacity, columns), (rows, columns)],
        smem=(0,),
    )
    gots = [swap(s, "tp", k + 1) for k, s in enumerate(sends)]
    grad, total, *sends = call(
        functools.partial(combine_kernel, enc, tp),
        (
            struct((rows, width), F32),
            struct((chunks, LANES), F32),
            *[struct((chunks + capacity * columns // LANES, LANES), F32)] * (enc - 1),
        ),
        (vis, bias, gain, inv_rms, kv, dots, own, *gots),
        scratch=[(rows, width)],
    )
    gots = [swap(s, "enc", k + 1) for k, s in enumerate(sends)]
    (visual_grad,) = call(round_kernel, (struct((buckets, capacity, width), BF16),), (grad,))
    add = functools.partial(sum_kernel, chunks)
    (total,) = call(add, (struct((chunks, LANES), F32),), (total, *gots))
    others = [swap(total, "llm", k) for k in range(1, llm)]
    (key_values,) = call(
        functools.partial(keys_kernel, enc),
        (struct((buckets, capacity, columns), BF16),),
        (kv, *gots),
    )
    (bias_grad,) = call(add, (struct((chunks, LANES), F32),), (total, *others))
    return (key_values[None, None], visual_grad[None, None], bias_grad.reshape(width))


def solution(mesh):
    return jax.shard_map(
        per_device,
        mesh=mesh,
        in_specs=(
            P("enc", "llm", None, None, None),
            P("enc", "llm", None),
            P(),
            P(),
            P(None, "tp"),
            P("enc", "llm", None, None, "tp"),
        ),
        out_specs=(P("enc", "llm", None, None, "tp"), P("enc", "llm", None, None, "tp"), P("tp")),
        check_vma=False,
    )
```

```python
import functools

import jax
import jax.numpy as jnp
from jax import lax
from jax.experimental import pallas as pl
from jax.experimental.pallas import tpu as pltpu
from jax.sharding import PartitionSpec as P

LANES = 128
PIECES = 3
VMEM = pl.BlockSpec(memory_space=pltpu.VMEM)
SMEM = pl.BlockSpec(memory_space=pltpu.SMEM)
HBM = pl.BlockSpec(memory_space=pltpu.HBM)
F32 = jnp.float32
BF16 = jnp.bfloat16


def swap(x, axis, k):
    n = lax.axis_size(axis)
    return lax.ppermute(x, axis, [(i, i ^ k) for i in range(n)])


def call(limit, kernel, outs, args, scratch=(), specs=None):
    return pl.pallas_call(
        kernel,
        out_shape=tuple(outs),
        in_specs=specs or [VMEM] * len(args),
        out_specs=tuple(VMEM for _ in outs),
        scratch_shapes=list(scratch),
        compiler_params=pltpu.CompilerParams(vmem_limit_bytes=limit),
    )(*args)


def norm_kernel(
    vis_hbm, bias_hbm, gain_hbm, cot_hbm, _, cot_ref, vis_ref, bias_ref, gain_ref,
    normed_ref, inv_ref, rows_ref, sems,
):
    pairs = [(cot_hbm, cot_ref), (vis_hbm, vis_ref), (bias_hbm, bias_ref), (gain_hbm, gain_ref)]
    copies = [pltpu.make_async_copy(a, b, sems.at[i]) for i, (a, b) in enumerate(pairs)]
    for copy in copies:
        copy.start()
    for copy in copies:
        copy.wait()
    buckets, capacity, features = vis_ref.shape
    for q in range(buckets):
        rows_ref[q * capacity : (q + 1) * capacity, :] = vis_ref[q].astype(F32) + bias_ref[...]
    inputs = rows_ref[...]
    mean = jnp.sum(inputs * inputs, axis=1, keepdims=True) / features
    inv_rms = lax.rsqrt(mean + 1e-06)
    normed_ref[...] = (inputs * inv_rms * gain_ref[...]).astype(BF16)
    inv_ref[...] = jnp.broadcast_to(inv_rms, inv_ref.shape)


def project_kernel(normed_ref, weight_ref, projected_ref):
    projected_ref[...] = jnp.dot(normed_ref[...], weight_ref[...], preferred_element_type=F32)


def split(value, dtype):
    if dtype == F32:
        return [value]
    pieces = []
    for _ in range(PIECES):
        pieces.append(value.astype(dtype))
        value = value - pieces[-1].astype(F32)
    return pieces


def side(count, rows, dtype):
    return LANES + len(split_shape(dtype)) * -(-count // rows) * LANES


def split_shape(dtype):
    return range(1 if dtype == F32 else PIECES)


def put_side(send_ref, start, dots, row, at, count):
    rows, dtype = send_ref.shape[0], send_ref.dtype
    if dots is not None:
        lane = lax.broadcasted_iota(jnp.int32, dots.shape, 1)
        block = jnp.zeros(dots.shape, F32)
        for i, piece in enumerate(split(dots, dtype)):
            block = jnp.where(lane == i, piece.astype(F32), block)
        send_ref[:, start : start + LANES] = block.astype(dtype)
    blocks = (send_ref.shape[1] - start) // LANES - 1
    blocks //= len(split_shape(dtype))
    for i, piece in enumerate(split(row, dtype)):
        for j in range(count):
            line, col = (at + j) % rows, start + LANES * (1 + i * blocks + (at + j) // rows)
            send_ref[line : line + 1, col : col + LANES] = piece[:, j * LANES : (j + 1) * LANES]


def get_dots(got_ref, start):
    return jnp.sum(got_ref[:, start : start + LANES].astype(F32), axis=1, keepdims=True)


def get_side(got_ref, start, at, count):
    rows, dtype = got_ref.shape[0], got_ref.dtype
    blocks = (got_ref.shape[1] - start) // LANES - 1
    blocks //= len(split_shape(dtype))
    out = []
    for j in range(0, count):
        line = (at + j) % rows
        total = None
        for i in split_shape(dtype):
            col = start + LANES * (1 + i * blocks + (at + j) // rows)
            piece = got_ref[line : line + 1, col : col + LANES].astype(F32)
            total = piece if total is None else total + piece
        out.append(total)
    return out


def products(k, tp, lhs_ref, weight_ref, vis_ref, bias_ref, gain_ref, inv_ref, dots_ref, rows_ref):
    buckets, capacity, features = vis_ref.shape
    width = features // tp
    place = lax.axis_index("tp")
    cols = pl.ds(pl.multiple_of((place ^ k) * width, width), width)
    term = lax.dot_general(
        lhs_ref[...], weight_ref[cols, :], (((1,), (1,)), ((), ())), preferred_element_type=F32
    )
    for q in range(buckets):
        rows_ref[q * capacity : (q + 1) * capacity, :] = (
            vis_ref[q, :, cols].astype(F32) + bias_ref[:, cols]
        )
    inv_rms = inv_ref[:, :1]
    scale = inv_rms * inv_rms * dots_ref[:, :1] / features
    row = gain_ref[:, cols] * jnp.sum(inv_rms * term, axis=0, keepdims=True)
    return term, row - jnp.sum(rows_ref[...] * scale, axis=0, keepdims=True)


def sent_kernel(enc, tp, counts_ref, projected_ref, weight_ref, vis_ref, bias_ref, gain_ref, inv_ref, *refs):
    cots = refs[:enc]
    kv_ref, dots_ref, lhs_ref, send_ref, picked_ref, masked_ref, rows_ref = refs[enc:]
    buckets, capacity, columns = kv_ref.shape
    me = lax.axis_index("enc")
    cots = cots[::-1]
    for k in range(enc):
        picked_ref[me ^ k] = cots[k][me].astype(F32)
    slot = lax.broadcasted_iota(jnp.int32, (capacity, columns), 0)
    for q in range(buckets):
        rows = slice(q * capacity, (q + 1) * capacity)
        live = slot < counts_ref[0, q]
        masked_ref[rows, :] = jnp.where(live, picked_ref[q], 0.0)
        kv_ref[q] = jnp.where(live, projected_ref[rows, :], 0.0)
    masked = masked_ref[...]
    dots = jnp.sum(masked * projected_ref[...], axis=1, keepdims=True)
    dots = jnp.broadcast_to(dots, dots_ref.shape)
    dots_ref[...] = dots
    lhs_ref[...] = masked.astype(BF16)
    width = vis_ref.shape[2] // tp
    chunks, half = width // LANES, tp // 2 * width
    for j in range(tp // 2):
        term, row = products(
            2 * j + 1, tp, lhs_ref, weight_ref, vis_ref, bias_ref, gain_ref, inv_ref, dots_ref, rows_ref
        )
        send_ref[:, j * width : (j + 1) * width] = term
        put_side(send_ref, half, None if j else dots, row, j * chunks, chunks)


def kept_kernel(tp, lhs_ref, weight_ref, vis_ref, bias_ref, gain_ref, inv_ref, dots_ref, kept_ref, sums_ref, rows_ref):
    width = vis_ref.shape[2] // tp
    chunks = width // LANES
    for j in range(tp // 2):
        term, row = products(
            2 * j, tp, lhs_ref, weight_ref, vis_ref, bias_ref, gain_ref, inv_ref, dots_ref, rows_ref
        )
        kept_ref[:, j * width : (j + 1) * width] = term
        for i in range(chunks):
            sums_ref[j * chunks + i : j * chunks + i + 1, :] = row[:, i * LANES : (i + 1) * LANES]


def fold_kernel(width, got_ref, kept_ref, dots_ref, sums_ref, all_ref, own_ref, *refs):
    pairs = kept_ref.shape[1] // width
    half, chunks = kept_ref.shape[1], width // LANES
    sends, totals = refs[: pairs - 1], refs[pairs - 1 :]
    dots = dots_ref[...] + get_dots(got_ref, half)
    all_ref[...] = dots
    for j in range(pairs):
        cols = slice(j * width, (j + 1) * width)
        term = kept_ref[:, cols] + got_ref[:, cols]
        for i, line in enumerate(get_side(got_ref, half, j * chunks, chunks)):
            row = sums_ref[j * chunks + i : j * chunks + i + 1, :] + line
            totals[j][i : i + 1, :] = row
            if j:
                put_side(sends[j - 1], width, None if i else dots, row, i, 1)
        if j:
            sends[j - 1][:, :width] = term.astype(BF16)
        else:
            own_ref[...] = term


def combine_kernel(enc, pairs, vis_ref, bias_ref, gain_ref, inv_ref, kv_ref, dots_ref, own_ref, sum_ref, *refs):
    gots, refs = refs[: pairs - 1], refs[pairs - 1 :]
    sums, refs = refs[: -enc - 2], refs[-enc - 2 :]
    grad_ref, total_ref = refs[:2]
    sends, rows_ref = refs[2:-1], refs[-1]
    buckets, capacity, features = vis_ref.shape
    width = own_ref.shape[1]
    chunks = width // LANES
    me, place = lax.axis_index("enc"), lax.axis_index("tp")
    own = pl.ds(pl.multiple_of(place * width, width), width)
    total = sum_ref[...]
    for got in sums:
        total = total + got[...]
    total_ref[...] = total
    for got in gots:
        for i, line in enumerate(get_side(got, width, 0, chunks)):
            total_ref[i : i + 1, :] = total_ref[i : i + 1, :] + line
    for k in range(1, enc):
        sends[k - 1][:chunks, :] = total_ref[...]
        block = kv_ref[me ^ k]
        for j in range(block.shape[1] // LANES):
            at = chunks + j * capacity
            sends[k - 1][at : at + capacity, :] = block[:, j * LANES : (j + 1) * LANES]
    for q in range(buckets):
        rows_ref[q * capacity : (q + 1) * capacity, :] = (
            vis_ref[q, :, own].astype(F32) + bias_ref[:, own]
        )
    grad_normed, row_dot = own_ref[...], dots_ref[:, :1]
    for got in gots:
        grad_normed = grad_normed + got[:, :width].astype(F32)
        row_dot = row_dot + get_dots(got, width)
    inv_rms = inv_ref[:, :1]
    grad_ref[...] = (
        inv_rms * gain_ref[:, own] * grad_normed
        - rows_ref[...] * (inv_rms * inv_rms) * row_dot / features
    )


def round_kernel(grad_ref, out_ref):
    buckets, capacity, _ = out_ref.shape
    for q in range(buckets):
        out_ref[q] = grad_ref[q * capacity : (q + 1) * capacity, :].astype(BF16)


def final_kernel(enc, total_ref, kv_ref, *refs):
    gots, (sum_ref, out_ref) = refs[: enc - 1][::-1], refs[enc - 1 :]
    buckets, capacity, columns = kv_ref.shape
    chunks = total_ref.shape[0]
    me = lax.axis_index("enc")
    total = total_ref[...]
    for got in gots:
        total = total + got[:chunks, :]
    sum_ref[...] = total
    out_ref[me] = kv_ref[me].astype(BF16)
    for k in range(1, enc):
        for j in range(columns // LANES):
            at = chunks + j * capacity
            out_ref[me ^ k, :, j * LANES : (j + 1) * LANES] = gots[k - 1][
                at : at + capacity, :
            ].astype(BF16)


def per_device(visual, counts, merger_bias, norm_gain, kv_weight, kv_cotangent):
    buckets, capacity, features = visual.shape[2:]
    enc, llm, tp = (lax.axis_size(a) for a in ("enc", "llm", "tp"))
    width, columns, rows = features // tp, kv_weight.shape[1], buckets * capacity
    chunks, pairs = width // LANES, tp // 2
    half = pairs * width
    part = functools.partial
    struct = jax.ShapeDtypeStruct
    run = part(call, 2 * kv_weight.size * 2 + 16 * rows * features)

    vis, bias, gain, cot = visual[0, 0], merger_bias[None], norm_gain[None], kv_cotangent[0, 0]
    own_cot, vis, bias, gain, normed, inv_rms = run(
        norm_kernel,
        (
            *[struct(a.shape, a.dtype) for a in (cot, vis, bias, gain)],
            struct((rows, features), BF16),
            struct((rows, LANES), F32),
        ),
        [
            pltpu.with_memory_space_constraint(a, pltpu.HBM)
            for a in (vis, bias, gain, cot, kv_weight)
        ],
        scratch=[pltpu.VMEM((rows, features), F32), pltpu.SemaphoreType.DMA((4,))],
        specs=[HBM] * 5,
    )
    cots = [own_cot] + [swap(own_cot, "enc", k) for k in range(1, enc)]
    (projected,) = run(project_kernel, (struct((rows, columns), F32),), (normed, kv_weight))
    kv, dots, lhs, send = run(
        part(sent_kernel, enc, tp),
        (
            struct((buckets, capacity, columns), F32),
            struct((rows, LANES), F32),
            struct((rows, columns), BF16),
            struct((rows, half + side(pairs * chunks, rows, F32)), F32),
        ),
        (counts[0], projected, kv_weight, vis, bias, gain, inv_rms, *cots[::-1]),
        scratch=[
            pltpu.VMEM((buckets, capacity, columns), F32),
            pltpu.VMEM((rows, columns), F32),
            pltpu.VMEM((rows, width), F32),
        ],
        specs=[SMEM, *[VMEM] * (6 + enc)],
    )
    got = swap(send, "tp", 1)
    kept, sums = run(
        part(kept_kernel, tp),
        (struct((rows, half), F32), struct((pairs * chunks, LANES), F32)),
        (lhs, kv_weight, vis, bias, gain, inv_rms, dots),
        scratch=[pltpu.VMEM((rows, width), F32)],
    )
    dots, own, *refs = run(
        part(fold_kernel, width),
        (
            struct((rows, LANES), F32),
            struct((rows, width), F32),
            *[struct((rows, width + side(chunks, rows, BF16)), BF16)] * (pairs - 1),
            *[struct((chunks, LANES), F32)] * pairs,
        ),
        (got, kept, dots, sums),
    )
    sends, totals = refs[: pairs - 1], refs[pairs - 1 :]
    gots = [swap(s, "tp", 2 * (j + 1)) for j, s in enumerate(sends)]
    others = [
        swap(t, ("llm", "tp"), tp * g + 2 * j) for g in range(1, llm) for j, t in enumerate(totals)
    ]
    grad, total, *sends = run(
        part(combine_kernel, enc, pairs),
        (
            struct((rows, width), F32),
            struct((chunks, LANES), F32),
            *[struct((chunks + capacity * columns // LANES, LANES), F32)] * (enc - 1),
        ),
        (vis, bias, gain, inv_rms, kv, dots, own, totals[0], *gots, *others),
        scratch=[pltpu.VMEM((rows, width), F32)],
    )
    gots = [swap(s, "enc", k + 1) for k, s in enumerate(sends)]
    (visual_grad,) = run(round_kernel, (struct((buckets, capacity, width), BF16),), (grad,))
    bias_grad, key_values = run(
        part(final_kernel, enc),
        (struct((chunks, LANES), F32), struct((buckets, capacity, columns), BF16)),
        (total, kv, *gots[::-1]),
    )
    return (key_values[None, None], visual_grad[None, None], bias_grad.reshape(width))


def solution(mesh):
    return jax.shard_map(
        per_device,
        mesh=mesh,
        in_specs=(
            P("enc", "llm", None, None, None),
            P("enc", "llm", None),
            P(),
            P(),
            P(None, "tp"),
            P("enc", "llm", None, None, "tp"),
        ),
        out_specs=(P("enc", "llm", None, None, "tp"), P("enc", "llm", None, None, "tp"), P("tp")),
        check_vma=False,
    )
```

```python
import functools

import jax
import jax.numpy as jnp
from jax import lax
from jax.experimental import pallas as pl
from jax.experimental.pallas import tpu as pltpu
from jax.sharding import PartitionSpec as P

LANES = 128
PIECES = 3
VMEM = pl.BlockSpec(memory_space=pltpu.VMEM)
SMEM = pl.BlockSpec(memory_space=pltpu.SMEM)
HBM = pl.BlockSpec(memory_space=pltpu.HBM)
F32 = jnp.float32
BF16 = jnp.bfloat16


def swap(x, axis, k):
    n = lax.axis_size(axis)
    return lax.ppermute(x, axis, [(i, i ^ k) for i in range(n)])


def call(limit, kernel, outs, args, scratch=(), specs=None):
    return pl.pallas_call(
        kernel,
        out_shape=tuple(outs),
        in_specs=specs or [VMEM] * len(args),
        out_specs=tuple(VMEM for _ in outs),
        scratch_shapes=list(scratch),
        compiler_params=pltpu.CompilerParams(vmem_limit_bytes=limit),
    )(*args)


def norm_kernel(
    vis_hbm, bias_hbm, gain_hbm, cot_hbm, _, cot_ref, vis_ref, bias_ref, gain_ref,
    normed_ref, inv_ref, rows_ref, sems,
):
    pairs = [(cot_hbm, cot_ref), (vis_hbm, vis_ref), (bias_hbm, bias_ref), (gain_hbm, gain_ref)]
    copies = [pltpu.make_async_copy(a, b, sems.at[i]) for i, (a, b) in enumerate(pairs)]
    for copy in copies:
        copy.start()
    for copy in copies:
        copy.wait()
    buckets, capacity, features = vis_ref.shape
    for q in range(buckets):
        rows_ref[q * capacity : (q + 1) * capacity, :] = vis_ref[q].astype(F32) + bias_ref[...]
    inputs = rows_ref[...]
    mean = jnp.sum(inputs * inputs, axis=1, keepdims=True) / features
    inv_rms = lax.rsqrt(mean + 1e-06)
    normed_ref[...] = (inputs * inv_rms * gain_ref[...]).astype(BF16)
    inv_ref[...] = jnp.broadcast_to(inv_rms, inv_ref.shape)


def project_kernel(normed_ref, weight_ref, projected_ref):
    projected_ref[...] = jnp.dot(normed_ref[...], weight_ref[...], preferred_element_type=F32)


def split(value, dtype):
    if dtype == F32:
        return [value]
    pieces = []
    for _ in range(PIECES):
        pieces.append(value.astype(dtype))
        value = value - pieces[-1].astype(F32)
    return pieces


def side(count, rows, dtype):
    return LANES + len(split_shape(dtype)) * -(-count // rows) * LANES


def split_shape(dtype):
    return range(1 if dtype == F32 else PIECES)


def put_side(send_ref, start, dots, row, at, count):
    rows, dtype = send_ref.shape[0], send_ref.dtype
    if dots is not None:
        lane = lax.broadcasted_iota(jnp.int32, dots.shape, 1)
        block = jnp.zeros(dots.shape, F32)
        for i, piece in enumerate(split(dots, dtype)):
            block = jnp.where(lane == i, piece.astype(F32), block)
        send_ref[:, start : start + LANES] = block.astype(dtype)
    blocks = (send_ref.shape[1] - start) // LANES - 1
    blocks //= len(split_shape(dtype))
    for i, piece in enumerate(split(row, dtype)):
        for j in range(count):
            line, col = (at + j) % rows, start + LANES * (1 + i * blocks + (at + j) // rows)
            send_ref[line : line + 1, col : col + LANES] = piece[:, j * LANES : (j + 1) * LANES]


def get_dots(got_ref, start):
    return jnp.sum(got_ref[:, start : start + LANES].astype(F32), axis=1, keepdims=True)


def get_side(got_ref, start, at, count):
    rows, dtype = got_ref.shape[0], got_ref.dtype
    blocks = (got_ref.shape[1] - start) // LANES - 1
    blocks //= len(split_shape(dtype))
    out = []
    for j in range(0, count):
        line = (at + j) % rows
        total = None
        for i in split_shape(dtype):
            col = start + LANES * (1 + i * blocks + (at + j) // rows)
            piece = got_ref[line : line + 1, col : col + LANES].astype(F32)
            total = piece if total is None else total + piece
        out.append(total)
    return out


def products(k, tp, lhs_ref, weight_ref, vis_ref, bias_ref, gain_ref, inv_ref, dots_ref, rows_ref):
    buckets, capacity, features = vis_ref.shape
    width = features // tp
    place = lax.axis_index("tp")
    cols = pl.ds(pl.multiple_of((place ^ k) * width, width), width)
    term = lax.dot_general(
        lhs_ref[...], weight_ref[cols, :], (((1,), (1,)), ((), ())), preferred_element_type=F32
    )
    for q in range(buckets):
        rows_ref[q * capacity : (q + 1) * capacity, :] = (
            vis_ref[q, :, cols].astype(F32) + bias_ref[:, cols]
        )
    inv_rms = inv_ref[:, :1]
    scale = inv_rms * inv_rms * dots_ref[:, :1] / features
    row = gain_ref[:, cols] * jnp.sum(inv_rms * term, axis=0, keepdims=True)
    return term, row - jnp.sum(rows_ref[...] * scale, axis=0, keepdims=True)


def sent_kernel(enc, tp, counts_ref, projected_ref, weight_ref, vis_ref, bias_ref, gain_ref, inv_ref, *refs):
    cots = refs[:enc]
    kv_ref, dots_ref, lhs_ref, send_ref, picked_ref, masked_ref, rows_ref = refs[enc:]
    buckets, capacity, columns = kv_ref.shape
    me = lax.axis_index("enc")
    cots = cots[::-1]
    for k in range(enc):
        picked_ref[me ^ k] = cots[k][me].astype(F32)
    slot = lax.broadcasted_iota(jnp.int32, (capacity, columns), 0)
    for q in range(buckets):
        rows = slice(q * capacity, (q + 1) * capacity)
        live = slot < counts_ref[0, q]
        masked_ref[rows, :] = jnp.where(live, picked_ref[q], 0.0)
        kv_ref[q] = jnp.where(live, projected_ref[rows, :], 0.0)
    masked = masked_ref[...]
    dots = jnp.sum(masked * projected_ref[...], axis=1, keepdims=True)
    dots = jnp.broadcast_to(dots, dots_ref.shape)
    dots_ref[...] = dots
    lhs_ref[...] = masked.astype(BF16)
    width = vis_ref.shape[2] // tp
    chunks, half = width // LANES, tp // 2 * width
    for j in range(tp // 2):
        term, row = products(
            2 * j + 1, tp, lhs_ref, weight_ref, vis_ref, bias_ref, gain_ref, inv_ref, dots_ref, rows_ref
        )
        send_ref[:, j * width : (j + 1) * width] = term
        put_side(send_ref, half, None if j else dots, row, j * chunks, chunks)


def kept_kernel(tp, lhs_ref, weight_ref, vis_ref, bias_ref, gain_ref, inv_ref, dots_ref, kept_ref, sums_ref, rows_ref):
    width = vis_ref.shape[2] // tp
    chunks = width // LANES
    for j in range(tp // 2):
        term, row = products(
            2 * j, tp, lhs_ref, weight_ref, vis_ref, bias_ref, gain_ref, inv_ref, dots_ref, rows_ref
        )
        kept_ref[:, j * width : (j + 1) * width] = term
        for i in range(chunks):
            sums_ref[j * chunks + i : j * chunks + i + 1, :] = row[:, i * LANES : (i + 1) * LANES]


def fold_kernel(width, got_ref, kept_ref, dots_ref, sums_ref, all_ref, own_ref, *refs):
    pairs = kept_ref.shape[1] // width
    half, chunks = kept_ref.shape[1], width // LANES
    sends, totals = refs[: pairs - 1], refs[pairs - 1 :]
    dots = dots_ref[...] + get_dots(got_ref, half)
    all_ref[...] = dots
    for j in range(pairs):
        cols = slice(j * width, (j + 1) * width)
        term = kept_ref[:, cols] + got_ref[:, cols]
        for i, line in enumerate(get_side(got_ref, half, j * chunks, chunks)):
            row = sums_ref[j * chunks + i : j * chunks + i + 1, :] + line
            totals[j][i : i + 1, :] = row
            if j:
                put_side(sends[j - 1], width, None if i else dots, row, i, 1)
        if j:
            sends[j - 1][:, :width] = term.astype(BF16)
        else:
            own_ref[...] = term


def combine_kernel(enc, pairs, vis_ref, bias_ref, gain_ref, inv_ref, kv_ref, dots_ref, own_ref, sum_ref, *refs):
    gots, refs = refs[: pairs - 1], refs[pairs - 1 :]
    sums, refs = refs[: -enc - 2], refs[-enc - 2 :]
    grad_ref, total_ref = refs[:2]
    sends, rows_ref = refs[2:-1], refs[-1]
    buckets, capacity, features = vis_ref.shape
    width = own_ref.shape[1]
    chunks = width // LANES
    me, place = lax.axis_index("enc"), lax.axis_index("tp")
    own = pl.ds(pl.multiple_of(place * width, width), width)
    total = sum_ref[...]
    for got in sums:
        total = total + got[...]
    total_ref[...] = total
    for got in gots:
        for i, line in enumerate(get_side(got, width, 0, chunks)):
            total_ref[i : i + 1, :] = total_ref[i : i + 1, :] + line
    for k in range(1, enc):
        sends[k - 1][:chunks, :] = total_ref[...]
        block = kv_ref[me ^ k]
        for j in range(block.shape[1] // LANES):
            at = chunks + j * capacity
            sends[k - 1][at : at + capacity, :] = block[:, j * LANES : (j + 1) * LANES]
    for q in range(buckets):
        rows_ref[q * capacity : (q + 1) * capacity, :] = (
            vis_ref[q, :, own].astype(F32) + bias_ref[:, own]
        )
    grad_normed, row_dot = own_ref[...], dots_ref[:, :1]
    for got in gots:
        grad_normed = grad_normed + got[:, :width].astype(F32)
        row_dot = row_dot + get_dots(got, width)
    inv_rms = inv_ref[:, :1]
    grad_ref[...] = (
        inv_rms * gain_ref[:, own] * grad_normed
        - rows_ref[...] * (inv_rms * inv_rms) * row_dot / features
    )


def round_kernel(grad_ref, out_ref):
    buckets, capacity, _ = out_ref.shape
    for q in range(buckets):
        out_ref[q] = grad_ref[q * capacity : (q + 1) * capacity, :].astype(BF16)


def final_kernel(enc, total_ref, kv_ref, *refs):
    gots, (sum_ref, out_ref) = refs[: enc - 1][::-1], refs[enc - 1 :]
    buckets, capacity, columns = kv_ref.shape
    chunks = total_ref.shape[0]
    me = lax.axis_index("enc")
    total = total_ref[...]
    for got in gots:
        total = total + got[:chunks, :]
    sum_ref[...] = total
    out_ref[me] = kv_ref[me].astype(BF16)
    for k in range(1, enc):
        for j in range(columns // LANES):
            at = chunks + j * capacity
            out_ref[me ^ k, :, j * LANES : (j + 1) * LANES] = gots[k - 1][
                at : at + capacity, :
            ].astype(BF16)


def per_device(visual, counts, merger_bias, norm_gain, kv_weight, kv_cotangent):
    buckets, capacity, features = visual.shape[2:]
    enc, llm, tp = (lax.axis_size(a) for a in ("enc", "llm", "tp"))
    width, columns, rows = features // tp, kv_weight.shape[1], buckets * capacity
    chunks, pairs = width // LANES, tp // 2
    half = pairs * width
    part = functools.partial
    struct = jax.ShapeDtypeStruct
    run = part(call, 2 * kv_weight.size * 2 + 16 * rows * features)

    vis, bias, gain, cot = visual[0, 0], merger_bias[None], norm_gain[None], kv_cotangent[0, 0]
    own_cot, vis, bias, gain, normed, inv_rms = run(
        norm_kernel,
        (
            *[struct(a.shape, a.dtype) for a in (cot, vis, bias, gain)],
            struct((rows, features), BF16),
            struct((rows, LANES), F32),
        ),
        [
            pltpu.with_memory_space_constraint(a, pltpu.HBM)
            for a in (vis, bias, gain, cot, kv_weight)
        ],
        scratch=[pltpu.VMEM((rows, features), F32), pltpu.SemaphoreType.DMA((4,))],
        specs=[HBM] * 5,
    )
    cots = [own_cot] + [swap(cot, "enc", k) for k in range(1, enc)]
    (projected,) = run(project_kernel, (struct((rows, columns), F32),), (normed, kv_weight))
    kv, dots, lhs, send = run(
        part(sent_kernel, enc, tp),
        (
            struct((buckets, capacity, columns), F32),
            struct((rows, LANES), F32),
            struct((rows, columns), BF16),
            struct((rows, half + side(pairs * chunks, rows, F32)), F32),
        ),
        (counts[0], projected, kv_weight, vis, bias, gain, inv_rms, *cots[::-1]),
        scratch=[
            pltpu.VMEM((buckets, capacity, columns), F32),
            pltpu.VMEM((rows, columns), F32),
            pltpu.VMEM((rows, width), F32),
        ],
        specs=[SMEM, *[VMEM] * (6 + enc)],
    )
    got = swap(send, "tp", 1)
    kept, sums = run(
        part(kept_kernel, tp),
        (struct((rows, half), F32), struct((pairs * chunks, LANES), F32)),
        (lhs, kv_weight, vis, bias, gain, inv_rms, dots),
        scratch=[pltpu.VMEM((rows, width), F32)],
    )
    dots, own, *refs = run(
        part(fold_kernel, width),
        (
            struct((rows, LANES), F32),
            struct((rows, width), F32),
            *[struct((rows, width + side(chunks, rows, BF16)), BF16)] * (pairs - 1),
            *[struct((chunks, LANES), F32)] * pairs,
        ),
        (got, kept, dots, sums),
    )
    sends, totals = refs[: pairs - 1], refs[pairs - 1 :]
    gots = [swap(s, "tp", 2 * (j + 1)) for j, s in enumerate(sends)]
    others = [
        swap(t, ("llm", "tp"), tp * g + 2 * j) for g in range(1, llm) for j, t in enumerate(totals)
    ]
    grad, total, *sends = run(
        part(combine_kernel, enc, pairs),
        (
            struct((rows, width), F32),
            struct((chunks, LANES), F32),
            *[struct((chunks + capacity * columns // LANES, LANES), F32)] * (enc - 1),
        ),
        (vis, bias, gain, inv_rms, kv, dots, own, totals[0], *gots, *others[::-1]),
        scratch=[pltpu.VMEM((rows, width), F32)],
    )
    gots = [swap(s, "enc", k + 1) for k, s in enumerate(sends)]
    (visual_grad,) = run(round_kernel, (struct((buckets, capacity, width), BF16),), (grad,))
    bias_grad, key_values = run(
        part(final_kernel, enc),
        (struct((chunks, LANES), F32), struct((buckets, capacity, columns), BF16)),
        (total, kv, *gots[::-1]),
    )
    return (key_values[None, None], visual_grad[None, None], bias_grad.reshape(width))


def solution(mesh):
    return jax.shard_map(
        per_device,
        mesh=mesh,
        in_specs=(
            P("enc", "llm", None, None, None),
            P("enc", "llm", None),
            P(),
            P(),
            P(None, "tp"),
            P("enc", "llm", None, None, "tp"),
        ),
        out_specs=(P("enc", "llm", None, None, "tp"), P("enc", "llm", None, None, "tp"), P("tp")),
        check_vma=False,
    )
```

```python
import functools

import jax
import jax.numpy as jnp
from jax import lax
from jax.experimental import pallas as pl
from jax.experimental.pallas import tpu as pltpu
from jax.sharding import PartitionSpec as P

LANES = 128
PIECES = 3
VMEM = pl.BlockSpec(memory_space=pltpu.VMEM)
SMEM = pl.BlockSpec(memory_space=pltpu.SMEM)
HBM = pl.BlockSpec(memory_space=pltpu.HBM)
F32 = jnp.float32
BF16 = jnp.bfloat16


def swap(x, axis, k):
    n = lax.axis_size(axis)
    return lax.ppermute(x, axis, [(i, i ^ k) for i in range(n)])


def call(limit, kernel, outs, args, scratch=(), specs=None):
    return pl.pallas_call(
        kernel,
        out_shape=tuple(outs),
        in_specs=specs or [VMEM] * len(args),
        out_specs=tuple(VMEM for _ in outs),
        scratch_shapes=list(scratch),
        compiler_params=pltpu.CompilerParams(vmem_limit_bytes=limit),
    )(*args)


def first_kernel(*refs):
    token_ref = refs[-1]
    token_ref[...] = jnp.zeros(token_ref.shape, F32)


def project_kernel(vis_ref, bias_ref, gain_ref, weight_ref, _, projected_ref, inv_ref, rows_ref, normed_ref):
    buckets, capacity, features = vis_ref.shape
    for q in range(buckets):
        rows_ref[q * capacity : (q + 1) * capacity, :] = vis_ref[q].astype(F32) + bias_ref[...]
    inputs = rows_ref[...]
    mean = jnp.sum(inputs * inputs, axis=1, keepdims=True) / features
    inv_rms = lax.rsqrt(mean + 1e-06)
    normed_ref[...] = (inputs * inv_rms * gain_ref[...]).astype(BF16)
    inv_ref[...] = jnp.broadcast_to(inv_rms, inv_ref.shape)
    projected_ref[...] = jnp.dot(normed_ref[...], weight_ref[...], preferred_element_type=F32)


def split(value, dtype):
    if dtype == F32:
        return [value]
    pieces = []
    for _ in range(PIECES):
        pieces.append(value.astype(dtype))
        value = value - pieces[-1].astype(F32)
    return pieces


def side(count, rows, dtype):
    return LANES + len(split_shape(dtype)) * -(-count // rows) * LANES


def split_shape(dtype):
    return range(1 if dtype == F32 else PIECES)


def put_side(send_ref, start, dots, row, at, count):
    rows, dtype = send_ref.shape[0], send_ref.dtype
    if dots is not None:
        lane = lax.broadcasted_iota(jnp.int32, dots.shape, 1)
        block = jnp.zeros(dots.shape, F32)
        for i, piece in enumerate(split(dots, dtype)):
            block = jnp.where(lane == i, piece.astype(F32), block)
        send_ref[:, start : start + LANES] = block.astype(dtype)
    blocks = (send_ref.shape[1] - start) // LANES - 1
    blocks //= len(split_shape(dtype))
    for i, piece in enumerate(split(row, dtype)):
        for j in range(count):
            line, col = (at + j) % rows, start + LANES * (1 + i * blocks + (at + j) // rows)
            send_ref[line : line + 1, col : col + LANES] = piece[:, j * LANES : (j + 1) * LANES]


def get_dots(got_ref, start):
    return jnp.sum(got_ref[:, start : start + LANES].astype(F32), axis=1, keepdims=True)


def get_side(got_ref, start, at, count):
    rows, dtype = got_ref.shape[0], got_ref.dtype
    blocks = (got_ref.shape[1] - start) // LANES - 1
    blocks //= len(split_shape(dtype))
    out = []
    for j in range(0, count):
        line = (at + j) % rows
        total = None
        for i in split_shape(dtype):
            col = start + LANES * (1 + i * blocks + (at + j) // rows)
            piece = got_ref[line : line + 1, col : col + LANES].astype(F32)
            total = piece if total is None else total + piece
        out.append(total)
    return out


def products(k, tp, lhs_ref, weight_ref, vis_ref, bias_ref, gain_ref, inv_ref, dots_ref, rows_ref):
    buckets, capacity, features = vis_ref.shape
    width = features // tp
    place = lax.axis_index("tp")
    cols = pl.ds(pl.multiple_of((place ^ k) * width, width), width)
    term = lax.dot_general(
        lhs_ref[...], weight_ref[cols, :], (((1,), (1,)), ((), ())), preferred_element_type=F32
    )
    for q in range(buckets):
        rows_ref[q * capacity : (q + 1) * capacity, :] = (
            vis_ref[q, :, cols].astype(F32) + bias_ref[:, cols]
        )
    inv_rms = inv_ref[:, :1]
    scale = inv_rms * inv_rms * dots_ref[:, :1] / features
    row = gain_ref[:, cols] * jnp.sum(inv_rms * term, axis=0, keepdims=True)
    return term, row - jnp.sum(rows_ref[...] * scale, axis=0, keepdims=True)


def sent_kernel(enc, tp, counts_ref, projected_ref, weight_ref, vis_ref, bias_ref, gain_ref, inv_ref, *refs):
    cots = refs[:enc]
    kv_ref, dots_ref, lhs_ref, send_ref, picked_ref, masked_ref, rows_ref = refs[enc:]
    buckets, capacity, columns = kv_ref.shape
    me = lax.axis_index("enc")
    cots = cots[::-1]
    for k in range(enc):
        picked_ref[me ^ k] = cots[k][me].astype(F32)
    slot = lax.broadcasted_iota(jnp.int32, (capacity, columns), 0)
    for q in range(buckets):
        rows = slice(q * capacity, (q + 1) * capacity)
        live = slot < counts_ref[0, q]
        masked_ref[rows, :] = jnp.where(live, picked_ref[q], 0.0)
        kv_ref[q] = jnp.where(live, projected_ref[rows, :], 0.0)
    masked = masked_ref[...]
    dots = jnp.sum(masked * projected_ref[...], axis=1, keepdims=True)
    dots = jnp.broadcast_to(dots, dots_ref.shape)
    dots_ref[...] = dots
    lhs_ref[...] = masked.astype(BF16)
    width = vis_ref.shape[2] // tp
    chunks, half = width // LANES, tp // 2 * width
    for j in range(tp // 2):
        term, row = products(
            2 * j + 1, tp, lhs_ref, weight_ref, vis_ref, bias_ref, gain_ref, inv_ref, dots_ref, rows_ref
        )
        send_ref[:, j * width : (j + 1) * width] = term
        put_side(send_ref, half, None if j else dots, row, j * chunks, chunks)


def kept_kernel(tp, lhs_ref, weight_ref, vis_ref, bias_ref, gain_ref, inv_ref, dots_ref, kept_ref, sums_ref, rows_ref):
    width = vis_ref.shape[2] // tp
    chunks = width // LANES
    for j in range(tp // 2):
        term, row = products(
            2 * j, tp, lhs_ref, weight_ref, vis_ref, bias_ref, gain_ref, inv_ref, dots_ref, rows_ref
        )
        kept_ref[:, j * width : (j + 1) * width] = term
        for i in range(chunks):
            sums_ref[j * chunks + i : j * chunks + i + 1, :] = row[:, i * LANES : (i + 1) * LANES]


def fold_kernel(width, got_ref, kept_ref, dots_ref, sums_ref, all_ref, own_ref, *refs):
    pairs = kept_ref.shape[1] // width
    half, chunks = kept_ref.shape[1], width // LANES
    sends, totals = refs[: pairs - 1], refs[pairs - 1 :]
    dots = dots_ref[...] + get_dots(got_ref, half)
    all_ref[...] = dots
    for j in range(pairs):
        cols = slice(j * width, (j + 1) * width)
        term = kept_ref[:, cols] + got_ref[:, cols]
        for i, line in enumerate(get_side(got_ref, half, j * chunks, chunks)):
            row = sums_ref[j * chunks + i : j * chunks + i + 1, :] + line
            totals[j][i : i + 1, :] = row
            if j:
                put_side(sends[j - 1], width, None if i else dots, row, i, 1)
        if j:
            sends[j - 1][:, :width] = term.astype(BF16)
        else:
            own_ref[...] = term


def combine_kernel(enc, pairs, vis_ref, bias_ref, gain_ref, inv_ref, kv_ref, dots_ref, own_ref, sum_ref, *refs):
    gots, refs = refs[: pairs - 1], refs[pairs - 1 :]
    sums, refs = refs[: -enc - 2], refs[-enc - 2 :]
    grad_ref, total_ref = refs[:2]
    sends, rows_ref = refs[2:-1], refs[-1]
    buckets, capacity, features = vis_ref.shape
    width = own_ref.shape[1]
    chunks = width // LANES
    me, place = lax.axis_index("enc"), lax.axis_index("tp")
    own = pl.ds(pl.multiple_of(place * width, width), width)
    total = sum_ref[...]
    for got in sums:
        total = total + got[...]
    total_ref[...] = total
    for got in gots:
        for i, line in enumerate(get_side(got, width, 0, chunks)):
            total_ref[i : i + 1, :] = total_ref[i : i + 1, :] + line
    for k in range(1, enc):
        sends[k - 1][:chunks, :] = total_ref[...]
        block = kv_ref[me ^ k]
        for j in range(block.shape[1] // LANES):
            at = chunks + j * capacity
            sends[k - 1][at : at + capacity, :] = block[:, j * LANES : (j + 1) * LANES]
    for q in range(buckets):
        rows_ref[q * capacity : (q + 1) * capacity, :] = (
            vis_ref[q, :, own].astype(F32) + bias_ref[:, own]
        )
    grad_normed, row_dot = own_ref[...], dots_ref[:, :1]
    for got in gots:
        grad_normed = grad_normed + got[:, :width].astype(F32)
        row_dot = row_dot + get_dots(got, width)
    inv_rms = inv_ref[:, :1]
    grad_ref[...] = (
        inv_rms * gain_ref[:, own] * grad_normed
        - rows_ref[...] * (inv_rms * inv_rms) * row_dot / features
    )


def round_kernel(grad_ref, out_ref):
    buckets, capacity, _ = out_ref.shape
    for q in range(buckets):
        out_ref[q] = grad_ref[q * capacity : (q + 1) * capacity, :].astype(BF16)


def final_kernel(enc, total_ref, kv_ref, *refs):
    gots, (sum_ref, out_ref) = refs[: enc - 1][::-1], refs[enc - 1 :]
    buckets, capacity, columns = kv_ref.shape
    chunks = total_ref.shape[0]
    me = lax.axis_index("enc")
    total = total_ref[...]
    for got in gots:
        total = total + got[:chunks, :]
    sum_ref[...] = total
    out_ref[me] = kv_ref[me].astype(BF16)
    for k in range(1, enc):
        for j in range(columns // LANES):
            at = chunks + j * capacity
            out_ref[me ^ k, :, j * LANES : (j + 1) * LANES] = gots[k - 1][
                at : at + capacity, :
            ].astype(BF16)


def per_device(visual, counts, merger_bias, norm_gain, kv_weight, kv_cotangent):
    buckets, capacity, features = visual.shape[2:]
    enc, llm, tp = (lax.axis_size(a) for a in ("enc", "llm", "tp"))
    width, columns, rows = features // tp, kv_weight.shape[1], buckets * capacity
    chunks, pairs = width // LANES, tp // 2
    half = pairs * width
    part = functools.partial
    struct = jax.ShapeDtypeStruct
    run = part(call, 2 * kv_weight.size * 2 + 16 * rows * features)

    vis, bias, gain, cot = visual[0, 0], merger_bias[None], norm_gain[None], kv_cotangent[0, 0]
    (token,) = run(
        first_kernel,
        (struct((8, LANES), F32),),
        [pltpu.with_memory_space_constraint(a, pltpu.HBM) for a in (kv_weight, vis, bias, gain)],
        specs=[HBM] * 4,
    )
    projected, inv_rms = run(
        project_kernel,
        (struct((rows, columns), F32), struct((rows, LANES), F32)),
        (vis, bias, gain, kv_weight, token),
        scratch=[pltpu.VMEM((rows, features), F32), pltpu.VMEM((rows, features), BF16)],
    )
    own_cot = cot
    cots = [own_cot] + [swap(cot, "enc", k) for k in range(1, enc)]
    kv, dots, lhs, send = run(
        part(sent_kernel, enc, tp),
        (
            struct((buckets, capacity, columns), F32),
            struct((rows, LANES), F32),
            struct((rows, columns), BF16),
            struct((rows, half + side(pairs * chunks, rows, F32)), F32),
        ),
        (counts[0], projected, kv_weight, vis, bias, gain, inv_rms, *cots[::-1]),
        scratch=[
            pltpu.VMEM((buckets, capacity, columns), F32),
            pltpu.VMEM((rows, columns), F32),
            pltpu.VMEM((rows, width), F32),
        ],
        specs=[SMEM, *[VMEM] * (6 + enc)],
    )
    got = swap(send, "tp", 1)
    kept, sums = run(
        part(kept_kernel, tp),
        (struct((rows, half), F32), struct((pairs * chunks, LANES), F32)),
        (lhs, kv_weight, vis, bias, gain, inv_rms, dots),
        scratch=[pltpu.VMEM((rows, width), F32)],
    )
    dots, own, *refs = run(
        part(fold_kernel, width),
        (
            struct((rows, LANES), F32),
            struct((rows, width), F32),
            *[struct((rows, width + side(chunks, rows, BF16)), BF16)] * (pairs - 1),
            *[struct((chunks, LANES), F32)] * pairs,
        ),
        (got, kept, dots, sums),
    )
    sends, totals = refs[: pairs - 1], refs[pairs - 1 :]
    gots = [swap(s, "tp", 2 * (j + 1)) for j, s in enumerate(sends)]
    others = [
        swap(t, ("llm", "tp"), tp * g + 2 * j) for g in range(1, llm) for j, t in enumerate(totals)
    ]
    grad, total, *sends = run(
        part(combine_kernel, enc, pairs),
        (
            struct((rows, width), F32),
            struct((chunks, LANES), F32),
            *[struct((chunks + capacity * columns // LANES, LANES), F32)] * (enc - 1),
        ),
        (vis, bias, gain, inv_rms, kv, dots, own, totals[0], *gots, *others[::-1]),
        scratch=[pltpu.VMEM((rows, width), F32)],
    )
    gots = [swap(s, "enc", k + 1) for k, s in enumerate(sends)]
    (visual_grad,) = run(round_kernel, (struct((buckets, capacity, width), BF16),), (grad,))
    bias_grad, key_values = run(
        part(final_kernel, enc),
        (struct((chunks, LANES), F32), struct((buckets, capacity, columns), BF16)),
        (total, kv, *gots[::-1]),
    )
    return (key_values[None, None], visual_grad[None, None], bias_grad.reshape(width))


def solution(mesh):
    return jax.shard_map(
        per_device,
        mesh=mesh,
        in_specs=(
            P("enc", "llm", None, None, None),
            P("enc", "llm", None),
            P(),
            P(),
            P(None, "tp"),
            P("enc", "llm", None, None, "tp"),
        ),
        out_specs=(P("enc", "llm", None, None, "tp"), P("enc", "llm", None, None, "tp"), P("tp")),
        check_vma=False,
    )
```

```python
import functools

import jax
import jax.numpy as jnp
from jax import lax
from jax.experimental import pallas as pl
from jax.experimental.pallas import tpu as pltpu
from jax.sharding import PartitionSpec as P

LANES = 128
PIECES = 3
VMEM = pl.BlockSpec(memory_space=pltpu.VMEM)
HBM = pl.BlockSpec(memory_space=pltpu.HBM)
F32 = jnp.float32
BF16 = jnp.bfloat16


def swap(x, axis, k):
    n = lax.axis_size(axis)
    return lax.ppermute(x, axis, [(i, i ^ k) for i in range(n)])


def call(limit, kernel, outs, args, scratch=(), specs=None):
    return pl.pallas_call(
        kernel,
        out_shape=tuple(outs),
        in_specs=specs or [VMEM] * len(args),
        out_specs=tuple(VMEM for _ in outs),
        scratch_shapes=list(scratch),
        compiler_params=pltpu.CompilerParams(vmem_limit_bytes=limit),
    )(*args)


def first_kernel(*refs):
    token_ref = refs[-1]
    token_ref[...] = jnp.zeros(token_ref.shape, F32)


def project_kernel(vis_ref, bias_ref, gain_ref, weight_ref, _, projected_ref, inv_ref, rows_ref, normed_ref):
    buckets, capacity, features = vis_ref.shape
    for q in range(buckets):
        rows_ref[q * capacity : (q + 1) * capacity, :] = vis_ref[q].astype(F32) + bias_ref[...]
    inputs = rows_ref[...]
    mean = jnp.sum(inputs * inputs, axis=1, keepdims=True) / features
    inv_rms = lax.rsqrt(mean + 1e-06)
    normed_ref[...] = (inputs * inv_rms * gain_ref[...]).astype(BF16)
    inv_ref[...] = jnp.broadcast_to(inv_rms, inv_ref.shape)
    projected_ref[...] = jnp.dot(normed_ref[...], weight_ref[...], preferred_element_type=F32)


def kept(j):
    return 2 * j + (1 if j else 0)


def split(value, dtype):
    if dtype == F32:
        return [value]
    pieces = []
    for _ in range(PIECES):
        pieces.append(value.astype(dtype))
        value = value - pieces[-1].astype(F32)
    return pieces


def side(count, rows, dtype):
    return LANES + len(split_shape(dtype)) * -(-count // rows) * LANES


def split_shape(dtype):
    return range(1 if dtype == F32 else PIECES)


def put_side(send_ref, start, dots, row, at, count):
    rows, dtype = send_ref.shape[0], send_ref.dtype
    if dots is not None:
        lane = lax.broadcasted_iota(jnp.int32, dots.shape, 1)
        block = jnp.zeros(dots.shape, F32)
        for i, piece in enumerate(split(dots, dtype)):
            block = jnp.where(lane == i, piece.astype(F32), block)
        send_ref[:, start : start + LANES] = block.astype(dtype)
    blocks = (send_ref.shape[1] - start) // LANES - 1
    blocks //= len(split_shape(dtype))
    for i, piece in enumerate(split(row, dtype)):
        for j in range(count):
            line, col = (at + j) % rows, start + LANES * (1 + i * blocks + (at + j) // rows)
            send_ref[line : line + 1, col : col + LANES] = piece[:, j * LANES : (j + 1) * LANES]


def get_dots(got_ref, start):
    return jnp.sum(got_ref[:, start : start + LANES].astype(F32), axis=1, keepdims=True)


def get_side(got_ref, start, at, count):
    rows, dtype = got_ref.shape[0], got_ref.dtype
    blocks = (got_ref.shape[1] - start) // LANES - 1
    blocks //= len(split_shape(dtype))
    out = []
    for j in range(0, count):
        line = (at + j) % rows
        total = None
        for i in split_shape(dtype):
            col = start + LANES * (1 + i * blocks + (at + j) // rows)
            piece = got_ref[line : line + 1, col : col + LANES].astype(F32)
            total = piece if total is None else total + piece
        out.append(total)
    return out


def products(steps, tp, lhs, weight_ref, out_ref):
    width = weight_ref.shape[0] // tp
    place = lax.axis_index("tp")
    for j, k in enumerate(steps):
        cols = pl.ds(pl.multiple_of((place ^ k) * width, width), width)
        out_ref[:, j * width : (j + 1) * width] = lax.dot_general(
            lhs, weight_ref[cols, :], (((1,), (1,)), ((), ())), preferred_element_type=F32
        )


def row_sum(k, tp, term, vis_ref, bias_ref, gain_ref, inv_rms, dots):
    buckets, capacity, features = vis_ref.shape
    width = features // tp
    place = lax.axis_index("tp")
    cols = pl.ds(pl.multiple_of((place ^ k) * width, width), width)
    scale = inv_rms * inv_rms * dots * (1.0 / features)
    row = gain_ref[:, cols] * jnp.sum(inv_rms * term, axis=0, keepdims=True)
    for q in range(buckets):
        part = scale[q * capacity : (q + 1) * capacity]
        inputs = vis_ref[q, :, cols].astype(F32) + bias_ref[:, cols]
        row = row - jnp.sum(inputs * part, axis=0, keepdims=True)
    return row


def sent_kernel(enc, tp, counts_ref, projected_ref, weight_ref, vis_ref, bias_ref, gain_ref, inv_ref, *refs):
    cots = refs[:enc]
    kv_ref, dots_ref, lhs_ref, send_ref = refs[enc:]
    buckets, capacity, columns = kv_ref.shape
    me = lax.axis_index("enc")
    cots = cots[::-1]
    slot = lax.broadcasted_iota(jnp.int32, (capacity, columns), 0)
    blocks = [cot[me].astype(F32) for cot in cots]
    parts = []
    for q in range(buckets):
        block = blocks[0]
        for k in range(1, enc):
            block = jnp.where((me ^ k) == q, blocks[k], block)
        live = slot < counts_ref[:, q : q + 1]
        parts.append(jnp.where(live, block, 0.0))
        kv_ref[q] = jnp.where(live, projected_ref[q * capacity : (q + 1) * capacity, :], 0.0)
    masked = jnp.concatenate(parts, axis=0)
    lhs = masked.astype(BF16)
    lhs_ref[...] = lhs
    steps = [kept(j) ^ 1 for j in range(tp // 2)]
    products(steps, tp, lhs, weight_ref, send_ref)
    dots = jnp.sum(masked * projected_ref[...], axis=1, keepdims=True)
    dots_ref[...] = jnp.broadcast_to(dots, dots_ref.shape)
    width = vis_ref.shape[2] // tp
    chunks, half = width // LANES, tp // 2 * width
    inv_rms = inv_ref[:, :1]
    for j, k in enumerate(steps):
        term = send_ref[:, j * width : (j + 1) * width]
        row = row_sum(k, tp, term, vis_ref, bias_ref, gain_ref, inv_rms, dots)
        put_side(send_ref, half, None if j else dots_ref[...], row, j * chunks, chunks)


def kept_kernel(tp, lhs_ref, weight_ref, vis_ref, bias_ref, gain_ref, inv_ref, dots_ref, kept_ref, sums_ref):
    width = vis_ref.shape[2] // tp
    chunks = width // LANES
    steps = [kept(j) for j in range(tp // 2)]
    products(steps, tp, lhs_ref[...], weight_ref, kept_ref)
    for j, k in enumerate(steps):
        term = kept_ref[:, j * width : (j + 1) * width]
        row = row_sum(k, tp, term, vis_ref, bias_ref, gain_ref, inv_ref[:, :1], dots_ref[:, :1])
        for i in range(chunks):
            sums_ref[j * chunks + i : j * chunks + i + 1, :] = row[:, i * LANES : (i + 1) * LANES]


def fold_kernel(width, got_ref, kept_ref, dots_ref, sums_ref, all_ref, own_ref, *refs):
    pairs = kept_ref.shape[1] // width
    half, chunks = kept_ref.shape[1], width // LANES
    sends, totals = refs[: pairs - 1], refs[pairs - 1 :]
    dots = dots_ref[...] + get_dots(got_ref, half)
    all_ref[...] = dots
    for j in range(pairs):
        cols = slice(j * width, (j + 1) * width)
        term = kept_ref[:, cols] + got_ref[:, cols]
        for i, line in enumerate(get_side(got_ref, half, j * chunks, chunks)):
            row = sums_ref[j * chunks + i : j * chunks + i + 1, :] + line
            totals[j][i : i + 1, :] = row
            if j:
                put_side(sends[j - 1], width, None if i else dots, row, i, 1)
        if j:
            sends[j - 1][:, :width] = term.astype(BF16)
        else:
            own_ref[...] = term


def combine_kernel(enc, pairs, vis_ref, bias_ref, gain_ref, inv_ref, kv_ref, dots_ref, own_ref, sum_ref, *refs):
    gots, refs = refs[: pairs - 1], refs[pairs - 1 :]
    sums, refs = refs[: -enc - 2], refs[-enc - 2 :]
    grad_ref, total_ref = refs[:2]
    sends, rows_ref = refs[2:-1], refs[-1]
    buckets, capacity, features = vis_ref.shape
    width = own_ref.shape[1]
    chunks = width // LANES
    me, place = lax.axis_index("enc"), lax.axis_index("tp")
    own = pl.ds(pl.multiple_of(place * width, width), width)
    total = sum_ref[...]
    for got in sums:
        total = total + got[...]
    total_ref[...] = total
    for got in gots:
        for i, line in enumerate(get_side(got, width, 0, chunks)):
            total_ref[i : i + 1, :] = total_ref[i : i + 1, :] + line
    for k in range(1, enc):
        sends[k - 1][:chunks, :] = total_ref[...]
        block = kv_ref[me ^ k]
        for j in range(block.shape[1] // LANES):
            at = chunks + j * capacity
            sends[k - 1][at : at + capacity, :] = block[:, j * LANES : (j + 1) * LANES]
    for q in range(buckets):
        rows_ref[q * capacity : (q + 1) * capacity, :] = (
            vis_ref[q, :, own].astype(F32) + bias_ref[:, own]
        )
    grad_normed, row_dot = own_ref[...], dots_ref[:, :1]
    for got in gots:
        grad_normed = grad_normed + got[:, :width].astype(F32)
        row_dot = row_dot + get_dots(got, width)
    inv_rms = inv_ref[:, :1]
    grad_ref[...] = (
        inv_rms * gain_ref[:, own] * grad_normed
        - rows_ref[...] * (inv_rms * inv_rms) * row_dot / features
    )


def round_kernel(grad_ref, out_ref):
    buckets, capacity, _ = out_ref.shape
    for q in range(buckets):
        out_ref[q] = grad_ref[q * capacity : (q + 1) * capacity, :].astype(BF16)


def final_kernel(enc, total_ref, kv_ref, *refs):
    gots, (sum_ref, out_ref) = refs[: enc - 1][::-1], refs[enc - 1 :]
    buckets, capacity, columns = kv_ref.shape
    chunks = total_ref.shape[0]
    me = lax.axis_index("enc")
    total = total_ref[...]
    for got in gots:
        total = total + got[:chunks, :]
    sum_ref[...] = total
    out_ref[me] = kv_ref[me].astype(BF16)
    for k in range(1, enc):
        for j in range(columns // LANES):
            at = chunks + j * capacity
            out_ref[me ^ k, :, j * LANES : (j + 1) * LANES] = gots[k - 1][
                at : at + capacity, :
            ].astype(BF16)


def per_device(visual, counts, merger_bias, norm_gain, kv_weight, kv_cotangent):
    buckets, capacity, features = visual.shape[2:]
    enc, llm, tp = (lax.axis_size(a) for a in ("enc", "llm", "tp"))
    width, columns, rows = features // tp, kv_weight.shape[1], buckets * capacity
    chunks, pairs = width // LANES, tp // 2
    half = pairs * width
    part = functools.partial
    struct = jax.ShapeDtypeStruct
    run = part(call, 2 * kv_weight.size * 2 + 16 * rows * features)

    vis, bias, gain, cot = visual[0, 0], merger_bias[None], norm_gain[None], kv_cotangent[0, 0]
    (token,) = run(
        first_kernel,
        (struct((8, LANES), F32),),
        [pltpu.with_memory_space_constraint(a, pltpu.HBM) for a in (kv_weight, vis, bias, gain)],
        specs=[HBM] * 4,
    )
    projected, inv_rms = run(
        project_kernel,
        (struct((rows, columns), F32), struct((rows, LANES), F32)),
        (vis, bias, gain, kv_weight, token),
        scratch=[pltpu.VMEM((rows, features), F32), pltpu.VMEM((rows, features), BF16)],
    )
    own_cot = cot
    cots = [own_cot] + [swap(cot, "enc", k) for k in range(1, enc)]
    kv, dots, lhs, send = run(
        part(sent_kernel, enc, tp),
        (
            struct((buckets, capacity, columns), F32),
            struct((rows, LANES), F32),
            struct((rows, columns), BF16),
            struct((rows, half + side(pairs * chunks, rows, F32)), F32),
        ),
        (counts[0], projected, kv_weight, vis, bias, gain, inv_rms, *cots[::-1]),
    )
    got = swap(send, "tp", 1)
    terms, sums = run(
        part(kept_kernel, tp),
        (struct((rows, half), F32), struct((pairs * chunks, LANES), F32)),
        (lhs, kv_weight, vis, bias, gain, inv_rms, dots),
    )
    dots, own, *refs = run(
        part(fold_kernel, width),
        (
            struct((rows, LANES), F32),
            struct((rows, width), F32),
            *[struct((rows, width + side(chunks, rows, BF16)), BF16)] * (pairs - 1),
            *[struct((chunks, LANES), F32)] * pairs,
        ),
        (got, terms, dots, sums),
    )
    sends, totals = refs[: pairs - 1], refs[pairs - 1 :]
    gots = [swap(s, "tp", kept(j + 1)) for j, s in enumerate(sends)]
    others = [
        swap(t, ("llm", "tp"), tp * g + kept(j)) for g in range(1, llm) for j, t in enumerate(totals)
    ]
    grad, total, *sends = run(
        part(combine_kernel, enc, pairs),
        (
            struct((rows, width), F32),
            struct((chunks, LANES), F32),
            *[struct((chunks + capacity * columns // LANES, LANES), F32)] * (enc - 1),
        ),
        (vis, bias, gain, inv_rms, kv, dots, own, totals[0], *gots, *others[::-1]),
        scratch=[pltpu.VMEM((rows, width), F32)],
    )
    gots = [swap(s, "enc", k + 1) for k, s in enumerate(sends)]
    (visual_grad,) = run(round_kernel, (struct((buckets, capacity, width), BF16),), (grad,))
    bias_grad, key_values = run(
        part(final_kernel, enc),
        (struct((chunks, LANES), F32), struct((buckets, capacity, columns), BF16)),
        (total, kv, *gots[::-1]),
    )
    return (key_values[None, None], visual_grad[None, None], bias_grad.reshape(width))


def solution(mesh):
    return jax.shard_map(
        per_device,
        mesh=mesh,
        in_specs=(
            P("enc", "llm", None, None, None),
            P("enc", "llm", None),
            P(),
            P(),
            P(None, "tp"),
            P("enc", "llm", None, None, "tp"),
        ),
        out_specs=(P("enc", "llm", None, None, "tp"), P("enc", "llm", None, None, "tp"), P("tp")),
        check_vma=False,
    )
```

```python
import functools

import jax
import jax.numpy as jnp
from jax import lax
from jax.experimental import pallas as pl
from jax.experimental.pallas import tpu as pltpu
from jax.sharding import PartitionSpec as P

LANES = 128
PIECES = 3
VMEM = pl.BlockSpec(memory_space=pltpu.VMEM)
HBM = pl.BlockSpec(memory_space=pltpu.HBM)
F32 = jnp.float32
BF16 = jnp.bfloat16


def swap(x, axis, k):
    n = lax.axis_size(axis)
    return lax.ppermute(x, axis, [(i, i ^ k) for i in range(n)])


def call(limit, kernel, outs, args, scratch=(), specs=None):
    return pl.pallas_call(
        kernel,
        out_shape=tuple(outs),
        in_specs=specs or [VMEM] * len(args),
        out_specs=tuple(VMEM for _ in outs),
        scratch_shapes=list(scratch),
        compiler_params=pltpu.CompilerParams(vmem_limit_bytes=limit),
    )(*args)


def first_kernel(*refs):
    token_ref = refs[-1]
    token_ref[...] = jnp.zeros(token_ref.shape, F32)


def project_kernel(vis_ref, bias_ref, gain_ref, weight_ref, _, projected_ref, inv_ref, rows_ref, normed_ref):
    buckets, capacity, features = vis_ref.shape
    for q in range(buckets):
        rows_ref[q * capacity : (q + 1) * capacity, :] = vis_ref[q].astype(F32) + bias_ref[...]
    inputs = rows_ref[...]
    mean = jnp.sum(inputs * inputs, axis=1, keepdims=True) / features
    inv_rms = lax.rsqrt(mean + 1e-06)
    normed_ref[...] = (inputs * inv_rms * gain_ref[...]).astype(BF16)
    inv_ref[...] = jnp.broadcast_to(inv_rms, inv_ref.shape)
    projected_ref[...] = jnp.dot(normed_ref[...], weight_ref[...], preferred_element_type=F32)


def kept(j):
    return 2 * j + (1 if j else 0)


def split(value, dtype):
    if dtype == F32:
        return [value]
    pieces = []
    for _ in range(PIECES):
        pieces.append(value.astype(dtype))
        value = value - pieces[-1].astype(F32)
    return pieces


def side(count, rows, dtype):
    return LANES * (1 + (1 if dtype == F32 else PIECES) * -(-count // rows))


def put_side(send_ref, start, dots, lines):
    rows, dtype = send_ref.shape[0], send_ref.dtype
    lane = lax.broadcasted_iota(jnp.int32, dots.shape, 1)
    block = jnp.zeros(dots.shape, F32)
    for i, piece in enumerate(split(dots, dtype)):
        block = jnp.where(lane == i, piece.astype(F32), block)
    blocks = [block.astype(dtype)]
    spare = -lines.shape[0] % rows
    if spare:
        lines = jnp.concatenate([lines, jnp.zeros((spare, LANES), F32)], axis=0)
    for piece in split(lines, dtype):
        blocks += [piece[i : i + rows] for i in range(0, piece.shape[0], rows)]
    for i, block in enumerate(blocks):
        send_ref[:, start + i * LANES : start + (i + 1) * LANES] = block


def get_dots(got_ref, start):
    return jnp.sum(got_ref[:, start : start + LANES].astype(F32), axis=1, keepdims=True)


def get_lines(got_ref, start, count):
    rows = got_ref.shape[0]
    each = -(-count // rows)
    blocks = [got_ref[:, i : i + LANES].astype(F32) for i in range(start + LANES, got_ref.shape[1], LANES)]
    total = None
    for i in range(0, len(blocks), each):
        piece = blocks[i] if each == 1 else jnp.concatenate(blocks[i : i + each], axis=0)
        total = piece if total is None else total + piece
    return total[:count]


def products(steps, tp, lhs, weight_ref, out_ref):
    width = weight_ref.shape[0] // tp
    place = lax.axis_index("tp")
    for j, k in enumerate(steps):
        cols = pl.ds(pl.multiple_of((place ^ k) * width, width), width)
        out_ref[:, j * width : (j + 1) * width] = lax.dot_general(
            lhs, weight_ref[cols, :], (((1,), (1,)), ((), ())), preferred_element_type=F32
        )


def row_sum(k, tp, term, vis_ref, bias_ref, gain_ref, inv_rms, dots):
    buckets, capacity, features = vis_ref.shape
    width = features // tp
    place = lax.axis_index("tp")
    cols = pl.ds(pl.multiple_of((place ^ k) * width, width), width)
    scale = inv_rms * inv_rms * dots * (1.0 / features)
    row = gain_ref[:, cols] * jnp.sum(inv_rms * term, axis=0, keepdims=True)
    for q in range(buckets):
        part = scale[q * capacity : (q + 1) * capacity]
        inputs = vis_ref[q, :, cols].astype(F32) + bias_ref[:, cols]
        row = row - jnp.sum(inputs * part, axis=0, keepdims=True)
    return row


def sent_kernel(enc, tp, counts_ref, projected_ref, weight_ref, vis_ref, bias_ref, gain_ref, inv_ref, *refs):
    cots = refs[:enc]
    kv_ref, dots_ref, lhs_ref, send_ref, sums_ref = refs[enc:]
    buckets, capacity, columns = kv_ref.shape
    me = lax.axis_index("enc")
    cots = cots[::-1]
    slot = lax.broadcasted_iota(jnp.int32, (capacity, columns), 0)
    blocks = [cot[me].astype(F32) for cot in cots]
    parts = []
    for q in range(buckets):
        block = blocks[0]
        for k in range(1, enc):
            block = jnp.where((me ^ k) == q, blocks[k], block)
        live = slot < counts_ref[:, q : q + 1]
        parts.append(jnp.where(live, block, 0.0))
        kv_ref[q] = jnp.where(live, projected_ref[q * capacity : (q + 1) * capacity, :], 0.0)
    masked = jnp.concatenate(parts, axis=0)
    lhs = masked.astype(BF16)
    lhs_ref[...] = lhs
    steps = [kept(j) ^ 1 for j in range(tp // 2)]
    products(steps, tp, lhs, weight_ref, send_ref)
    dots = jnp.sum(masked * projected_ref[...], axis=1, keepdims=True)
    dots_ref[...] = jnp.broadcast_to(dots, dots_ref.shape)
    width = vis_ref.shape[2] // tp
    chunks, half = width // LANES, tp // 2 * width
    inv_rms = inv_ref[:, :1]
    for j, k in enumerate(steps):
        term = send_ref[:, j * width : (j + 1) * width]
        row = row_sum(k, tp, term, vis_ref, bias_ref, gain_ref, inv_rms, dots)
        for i in range(chunks):
            sums_ref[j * chunks + i : j * chunks + i + 1, :] = row[:, i * LANES : (i + 1) * LANES]
    put_side(send_ref, half, dots_ref[...], sums_ref[...])


def kept_kernel(tp, lhs_ref, weight_ref, vis_ref, bias_ref, gain_ref, inv_ref, dots_ref, kept_ref, sums_ref):
    width = vis_ref.shape[2] // tp
    chunks = width // LANES
    steps = [kept(j) for j in range(tp // 2)]
    products(steps, tp, lhs_ref[...], weight_ref, kept_ref)
    for j, k in enumerate(steps):
        term = kept_ref[:, j * width : (j + 1) * width]
        row = row_sum(k, tp, term, vis_ref, bias_ref, gain_ref, inv_ref[:, :1], dots_ref[:, :1])
        for i in range(chunks):
            sums_ref[j * chunks + i : j * chunks + i + 1, :] = row[:, i * LANES : (i + 1) * LANES]


def fold_kernel(width, got_ref, kept_ref, dots_ref, sums_ref, all_ref, own_ref, *refs):
    pairs = kept_ref.shape[1] // width
    half, chunks = kept_ref.shape[1], width // LANES
    sends, totals = refs[: pairs - 1], refs[pairs - 1 :]
    dots = dots_ref[...] + get_dots(got_ref, half)
    all_ref[...] = dots
    sums = sums_ref[...] + get_lines(got_ref, half, pairs * chunks)
    for j in range(pairs):
        cols = slice(j * width, (j + 1) * width)
        term = kept_ref[:, cols] + got_ref[:, cols]
        lines = sums[j * chunks : (j + 1) * chunks]
        totals[j][...] = lines
        if j:
            sends[j - 1][:, :width] = term.astype(BF16)
            put_side(sends[j - 1], width, dots, lines)
        else:
            own_ref[...] = term


def combine_kernel(enc, pairs, vis_ref, bias_ref, gain_ref, inv_ref, kv_ref, dots_ref, own_ref, sum_ref, *refs):
    gots, refs = refs[: pairs - 1], refs[pairs - 1 :]
    sums, refs = refs[: -enc - 2], refs[-enc - 2 :]
    grad_ref, total_ref = refs[:2]
    sends, rows_ref = refs[2:-1], refs[-1]
    buckets, capacity, features = vis_ref.shape
    width = own_ref.shape[1]
    chunks = width // LANES
    me, place = lax.axis_index("enc"), lax.axis_index("tp")
    own = pl.ds(pl.multiple_of(place * width, width), width)
    total = sum_ref[...]
    for got in sums:
        total = total + got[...]
    for got in gots:
        total = total + get_lines(got, width, chunks)
    total_ref[...] = total
    for k in range(1, enc):
        sends[k - 1][:chunks, :] = total
        block = kv_ref[me ^ k]
        for j in range(block.shape[1] // LANES):
            at = chunks + j * capacity
            sends[k - 1][at : at + capacity, :] = block[:, j * LANES : (j + 1) * LANES]
    for q in range(buckets):
        rows_ref[q * capacity : (q + 1) * capacity, :] = (
            vis_ref[q, :, own].astype(F32) + bias_ref[:, own]
        )
    grad_normed, row_dot = own_ref[...], dots_ref[:, :1]
    for got in gots:
        grad_normed = grad_normed + got[:, :width].astype(F32)
        row_dot = row_dot + get_dots(got, width)
    inv_rms = inv_ref[:, :1]
    grad_ref[...] = (
        inv_rms * gain_ref[:, own] * grad_normed
        - rows_ref[...] * (inv_rms * inv_rms) * row_dot / features
    )


def round_kernel(grad_ref, out_ref):
    buckets, capacity, _ = out_ref.shape
    for q in range(buckets):
        out_ref[q] = grad_ref[q * capacity : (q + 1) * capacity, :].astype(BF16)


def final_kernel(enc, total_ref, kv_ref, *refs):
    gots, (sum_ref, out_ref) = refs[: enc - 1][::-1], refs[enc - 1 :]
    buckets, capacity, columns = kv_ref.shape
    chunks = total_ref.shape[0]
    me = lax.axis_index("enc")
    total = total_ref[...]
    for got in gots:
        total = total + got[:chunks, :]
    sum_ref[...] = total
    out_ref[me] = kv_ref[me].astype(BF16)
    for k in range(1, enc):
        for j in range(columns // LANES):
            at = chunks + j * capacity
            out_ref[me ^ k, :, j * LANES : (j + 1) * LANES] = gots[k - 1][
                at : at + capacity, :
            ].astype(BF16)


def per_device(visual, counts, merger_bias, norm_gain, kv_weight, kv_cotangent):
    buckets, capacity, features = visual.shape[2:]
    enc, llm, tp = (lax.axis_size(a) for a in ("enc", "llm", "tp"))
    width, columns, rows = features // tp, kv_weight.shape[1], buckets * capacity
    chunks, pairs = width // LANES, tp // 2
    half = pairs * width
    part = functools.partial
    struct = jax.ShapeDtypeStruct
    run = part(call, 2 * kv_weight.size * 2 + 16 * rows * features)

    vis, bias, gain, cot = visual[0, 0], merger_bias[None], norm_gain[None], kv_cotangent[0, 0]
    (token,) = run(
        first_kernel,
        (struct((8, LANES), F32),),
        [pltpu.with_memory_space_constraint(a, pltpu.HBM) for a in (kv_weight, vis, bias, gain)],
        specs=[HBM] * 4,
    )
    projected, inv_rms = run(
        project_kernel,
        (struct((rows, columns), F32), struct((rows, LANES), F32)),
        (vis, bias, gain, kv_weight, token),
        scratch=[pltpu.VMEM((rows, features), F32), pltpu.VMEM((rows, features), BF16)],
    )
    own_cot = cot
    cots = [own_cot] + [swap(cot, "enc", k) for k in range(1, enc)]
    kv, dots, lhs, send = run(
        part(sent_kernel, enc, tp),
        (
            struct((buckets, capacity, columns), F32),
            struct((rows, LANES), F32),
            struct((rows, columns), BF16),
            struct((rows, half + side(pairs * chunks, rows, F32)), F32),
        ),
        (counts[0], projected, kv_weight, vis, bias, gain, inv_rms, *cots[::-1]),
        scratch=[pltpu.VMEM((pairs * chunks, LANES), F32)],
    )
    got = swap(send, "tp", 1)
    terms, sums = run(
        part(kept_kernel, tp),
        (struct((rows, half), F32), struct((pairs * chunks, LANES), F32)),
        (lhs, kv_weight, vis, bias, gain, inv_rms, dots),
    )
    dots, own, *refs = run(
        part(fold_kernel, width),
        (
            struct((rows, LANES), F32),
            struct((rows, width), F32),
            *[struct((rows, width + side(chunks, rows, BF16)), BF16)] * (pairs - 1),
            *[struct((chunks, LANES), F32)] * pairs,
        ),
        (got, terms, dots, sums),
    )
    sends, totals = refs[: pairs - 1], refs[pairs - 1 :]
    gots = [swap(s, "tp", kept(j + 1)) for j, s in enumerate(sends)]
    others = [
        swap(t, ("llm", "tp"), tp * g + kept(j)) for g in range(1, llm) for j, t in enumerate(totals)
    ]
    grad, total, *sends = run(
        part(combine_kernel, enc, pairs),
        (
            struct((rows, width), F32),
            struct((chunks, LANES), F32),
            *[struct((chunks + capacity * columns // LANES, LANES), F32)] * (enc - 1),
        ),
        (vis, bias, gain, inv_rms, kv, dots, own, totals[0], *gots, *others[::-1]),
        scratch=[pltpu.VMEM((rows, width), F32)],
    )
    gots = [swap(s, "enc", k + 1) for k, s in enumerate(sends)]
    (visual_grad,) = run(round_kernel, (struct((buckets, capacity, width), BF16),), (grad,))
    bias_grad, key_values = run(
        part(final_kernel, enc),
        (struct((chunks, LANES), F32), struct((buckets, capacity, columns), BF16)),
        (total, kv, *gots[::-1]),
    )
    return (key_values[None, None], visual_grad[None, None], bias_grad.reshape(width))


def solution(mesh):
    return jax.shard_map(
        per_device,
        mesh=mesh,
        in_specs=(
            P("enc", "llm", None, None, None),
            P("enc", "llm", None),
            P(),
            P(),
            P(None, "tp"),
            P("enc", "llm", None, None, "tp"),
        ),
        out_specs=(P("enc", "llm", None, None, "tp"), P("enc", "llm", None, None, "tp"), P("tp")),
        check_vma=False,
    )
```

```python
import functools

import jax
import jax.numpy as jnp
from jax import lax
from jax.experimental import pallas as pl
from jax.experimental.pallas import tpu as pltpu
from jax.sharding import PartitionSpec as P

LANES = 128
PIECES = 3
TERMS = 2
VMEM = pl.BlockSpec(memory_space=pltpu.VMEM)
HBM = pl.BlockSpec(memory_space=pltpu.HBM)
F32 = jnp.float32
BF16 = jnp.bfloat16


def swap(x, axis, k):
    n = lax.axis_size(axis)
    return lax.ppermute(x, axis, [(i, i ^ k) for i in range(n)])


def call(limit, kernel, outs, args, scratch=(), specs=None):
    return pl.pallas_call(
        kernel,
        out_shape=tuple(outs),
        in_specs=specs or [VMEM] * len(args),
        out_specs=tuple(VMEM for _ in outs),
        scratch_shapes=list(scratch),
        compiler_params=pltpu.CompilerParams(vmem_limit_bytes=limit),
    )(*args)


def first_kernel(*refs):
    token_ref = refs[-1]
    token_ref[...] = jnp.zeros(token_ref.shape, F32)


def project_kernel(vis_ref, bias_ref, gain_ref, weight_ref, _, projected_ref, inv_ref, rows_ref, normed_ref):
    buckets, capacity, features = vis_ref.shape
    for q in range(buckets):
        rows_ref[q * capacity : (q + 1) * capacity, :] = vis_ref[q].astype(F32) + bias_ref[...]
    inputs = rows_ref[...]
    mean = jnp.sum(inputs * inputs, axis=1, keepdims=True) / features
    inv_rms = lax.rsqrt(mean + 1e-06)
    normed_ref[...] = (inputs * inv_rms * gain_ref[...]).astype(BF16)
    inv_ref[...] = jnp.broadcast_to(inv_rms, inv_ref.shape)
    projected_ref[...] = jnp.dot(normed_ref[...], weight_ref[...], preferred_element_type=F32)


def kept(j):
    return 2 * j + (1 if j else 0)


def split(value, dtype):
    if dtype == F32:
        return [value]
    pieces = []
    for _ in range(PIECES):
        pieces.append(value.astype(dtype))
        value = value - pieces[-1].astype(F32)
    return pieces


def side(count, rows, dtype):
    return LANES * (1 + (1 if dtype == F32 else PIECES) * -(-count // rows))


def put_side(send_ref, start, dots, lines):
    rows, dtype = send_ref.shape[0], send_ref.dtype
    lane = lax.broadcasted_iota(jnp.int32, dots.shape, 1)
    block = jnp.zeros(dots.shape, F32)
    for i, piece in enumerate(split(dots, dtype)):
        block = jnp.where(lane == i, piece.astype(F32), block)
    blocks = [block.astype(dtype)]
    spare = -lines.shape[0] % rows
    if spare:
        lines = jnp.concatenate([lines, jnp.zeros((spare, LANES), F32)], axis=0)
    for piece in split(lines, dtype):
        blocks += [piece[i : i + rows] for i in range(0, piece.shape[0], rows)]
    for i, block in enumerate(blocks):
        send_ref[:, start + i * LANES : start + (i + 1) * LANES] = block


def get_dots(got_ref, start):
    return jnp.sum(got_ref[:, start : start + LANES].astype(F32), axis=1, keepdims=True)


def get_lines(got_ref, start, count):
    rows = got_ref.shape[0]
    each = -(-count // rows)
    blocks = [got_ref[:, i : i + LANES].astype(F32) for i in range(start + LANES, got_ref.shape[1], LANES)]
    total = None
    for i in range(0, len(blocks), each):
        piece = blocks[i] if each == 1 else jnp.concatenate(blocks[i : i + each], axis=0)
        total = piece if total is None else total + piece
    return total[:count]


def products(steps, tp, lhs, weight_ref, out_ref):
    width = weight_ref.shape[0] // tp
    place = lax.axis_index("tp")
    for j, k in enumerate(steps):
        cols = pl.ds(pl.multiple_of((place ^ k) * width, width), width)
        out_ref[:, j * width : (j + 1) * width] = lax.dot_general(
            lhs, weight_ref[cols, :], (((1,), (1,)), ((), ())), preferred_element_type=F32
        )


def row_sum(k, tp, term, vis_ref, bias_ref, gain_ref, inv_rms, dots):
    buckets, capacity, features = vis_ref.shape
    width = features // tp
    place = lax.axis_index("tp")
    cols = pl.ds(pl.multiple_of((place ^ k) * width, width), width)
    scale = inv_rms * inv_rms * dots * (1.0 / features)
    row = gain_ref[:, cols] * jnp.sum(inv_rms * term, axis=0, keepdims=True)
    for q in range(buckets):
        part = scale[q * capacity : (q + 1) * capacity]
        inputs = vis_ref[q, :, cols].astype(F32) + bias_ref[:, cols]
        row = row - jnp.sum(inputs * part, axis=0, keepdims=True)
    return row


def sent_kernel(enc, tp, counts_ref, projected_ref, weight_ref, vis_ref, bias_ref, gain_ref, inv_ref, *refs):
    cots = refs[:enc]
    kv_ref, dots_ref, lhs_ref, send_ref, sums_ref = refs[enc:]
    buckets, capacity, columns = kv_ref.shape
    me = lax.axis_index("enc")
    slot = lax.broadcasted_iota(jnp.int32, (capacity, columns), 0)
    blocks = [cot[me].astype(F32) for cot in cots]
    parts = []
    for q in range(buckets):
        block = blocks[0]
        for k in range(1, enc):
            block = jnp.where((me ^ k) == q, blocks[k], block)
        live = slot < counts_ref[:, q : q + 1]
        parts.append(jnp.where(live, block, 0.0))
        kv_ref[q] = jnp.where(live, projected_ref[q * capacity : (q + 1) * capacity, :], 0.0)
    masked = jnp.concatenate(parts, axis=0)
    lhs = masked.astype(BF16)
    lhs_ref[...] = lhs
    steps = [kept(j) ^ 1 for j in range(tp // 2)]
    products(steps, tp, lhs, weight_ref, send_ref)
    dots = jnp.sum(masked * projected_ref[...], axis=1, keepdims=True)
    dots_ref[...] = jnp.broadcast_to(dots, dots_ref.shape)
    width = vis_ref.shape[2] // tp
    chunks, half = width // LANES, tp // 2 * width
    inv_rms = inv_ref[:, :1]
    for j, k in enumerate(steps):
        term = send_ref[:, j * width : (j + 1) * width]
        row = row_sum(k, tp, term, vis_ref, bias_ref, gain_ref, inv_rms, dots)
        for i in range(chunks):
            sums_ref[j * chunks + i : j * chunks + i + 1, :] = row[:, i * LANES : (i + 1) * LANES]
    put_side(send_ref, half, dots_ref[...], sums_ref[...])


def kept_kernel(tp, lhs_ref, weight_ref, vis_ref, bias_ref, gain_ref, inv_ref, dots_ref, kept_ref, sums_ref):
    width = vis_ref.shape[2] // tp
    chunks = width // LANES
    steps = [kept(j) for j in range(tp // 2)]
    products(steps, tp, lhs_ref[...], weight_ref, kept_ref)
    for j, k in enumerate(steps):
        term = kept_ref[:, j * width : (j + 1) * width]
        row = row_sum(k, tp, term, vis_ref, bias_ref, gain_ref, inv_ref[:, :1], dots_ref[:, :1])
        for i in range(chunks):
            sums_ref[j * chunks + i : j * chunks + i + 1, :] = row[:, i * LANES : (i + 1) * LANES]


def fold_kernel(width, got_ref, kept_ref, dots_ref, sums_ref, all_ref, own_ref, *refs):
    pairs = kept_ref.shape[1] // width
    half, chunks = kept_ref.shape[1], width // LANES
    sends, totals = refs[: pairs - 1], refs[pairs - 1 :]
    dots = dots_ref[...] + get_dots(got_ref, half)
    all_ref[...] = dots
    sums = sums_ref[...] + get_lines(got_ref, half, pairs * chunks)
    for j in range(pairs):
        cols = slice(j * width, (j + 1) * width)
        term = kept_ref[:, cols] + got_ref[:, cols]
        lines = sums[j * chunks : (j + 1) * chunks]
        totals[j][...] = lines
        if j:
            for i in range(TERMS):
                piece = term.astype(BF16)
                sends[j - 1][:, i * width : (i + 1) * width] = piece
                term = term - piece.astype(F32)
            put_side(sends[j - 1], TERMS * width, dots, lines)
        else:
            own_ref[...] = term


def combine_kernel(enc, pairs, vis_ref, bias_ref, gain_ref, inv_ref, kv_ref, dots_ref, own_ref, sum_ref, *refs):
    gots, refs = refs[: pairs - 1], refs[pairs - 1 :]
    sums, refs = refs[: -enc - 2], refs[-enc - 2 :]
    grad_ref, total_ref = refs[:2]
    sends, rows_ref = refs[2:-1], refs[-1]
    buckets, capacity, features = vis_ref.shape
    width = own_ref.shape[1]
    chunks = width // LANES
    me, place = lax.axis_index("enc"), lax.axis_index("tp")
    own = pl.ds(pl.multiple_of(place * width, width), width)
    total = sum_ref[...]
    for got in sums:
        total = total + got[...]
    for got in gots:
        total = total + get_lines(got, TERMS * width, chunks)
    total_ref[...] = total
    for k in range(1, enc):
        sends[k - 1][:chunks, :] = total
        block = kv_ref[me ^ k]
        for j in range(block.shape[1] // LANES):
            at = chunks + j * capacity
            sends[k - 1][at : at + capacity, :] = block[:, j * LANES : (j + 1) * LANES]
    for q in range(buckets):
        rows_ref[q * capacity : (q + 1) * capacity, :] = (
            vis_ref[q, :, own].astype(F32) + bias_ref[:, own]
        )
    grad_normed, row_dot = own_ref[...], dots_ref[:, :1]
    for got in gots:
        for i in range(TERMS):
            grad_normed = grad_normed + got[:, i * width : (i + 1) * width].astype(F32)
        row_dot = row_dot + get_dots(got, TERMS * width)
    inv_rms = inv_ref[:, :1]
    grad_ref[...] = (
        inv_rms * gain_ref[:, own] * grad_normed
        - rows_ref[...] * (inv_rms * inv_rms) * row_dot / features
    )


def round_kernel(grad_ref, out_ref):
    buckets, capacity, _ = out_ref.shape
    for q in range(buckets):
        out_ref[q] = grad_ref[q * capacity : (q + 1) * capacity, :].astype(BF16)


def final_kernel(enc, total_ref, kv_ref, *refs):
    gots, (sum_ref, out_ref) = refs[: enc - 1][::-1], refs[enc - 1 :]
    buckets, capacity, columns = kv_ref.shape
    chunks = total_ref.shape[0]
    me = lax.axis_index("enc")
    total = total_ref[...]
    for got in gots:
        total = total + got[:chunks, :]
    sum_ref[...] = total
    out_ref[me] = kv_ref[me].astype(BF16)
    for k in range(1, enc):
        for j in range(columns // LANES):
            at = chunks + j * capacity
            out_ref[me ^ k, :, j * LANES : (j + 1) * LANES] = gots[k - 1][
                at : at + capacity, :
            ].astype(BF16)


def per_device(visual, counts, merger_bias, norm_gain, kv_weight, kv_cotangent):
    buckets, capacity, features = visual.shape[2:]
    enc, llm, tp = (lax.axis_size(a) for a in ("enc", "llm", "tp"))
    width, columns, rows = features // tp, kv_weight.shape[1], buckets * capacity
    chunks, pairs = width // LANES, tp // 2
    half = pairs * width
    part = functools.partial
    struct = jax.ShapeDtypeStruct
    run = part(call, 2 * kv_weight.size * 2 + 16 * rows * features)

    vis, bias, gain, cot = visual[0, 0], merger_bias[None], norm_gain[None], kv_cotangent[0, 0]
    (token,) = run(
        first_kernel,
        (struct((8, LANES), F32),),
        [pltpu.with_memory_space_constraint(a, pltpu.HBM) for a in (kv_weight, vis, bias, gain)],
        specs=[HBM] * 4,
    )
    projected, inv_rms = run(
        project_kernel,
        (struct((rows, columns), F32), struct((rows, LANES), F32)),
        (vis, bias, gain, kv_weight, token),
        scratch=[pltpu.VMEM((rows, features), F32), pltpu.VMEM((rows, features), BF16)],
    )
    own_cot = cot
    cots = [own_cot] + [swap(cot, "enc", k) for k in range(1, enc)]
    kv, dots, lhs, send = run(
        part(sent_kernel, enc, tp),
        (
            struct((buckets, capacity, columns), F32),
            struct((rows, LANES), F32),
            struct((rows, columns), BF16),
            struct((rows, half + side(pairs * chunks, rows, F32)), F32),
        ),
        (counts[0], projected, kv_weight, vis, bias, gain, inv_rms, *cots),
        scratch=[pltpu.VMEM((pairs * chunks, LANES), F32)],
    )
    got = swap(send, "tp", 1)
    terms, sums = run(
        part(kept_kernel, tp),
        (struct((rows, half), F32), struct((pairs * chunks, LANES), F32)),
        (lhs, kv_weight, vis, bias, gain, inv_rms, dots),
    )
    dots, own, *refs = run(
        part(fold_kernel, width),
        (
            struct((rows, LANES), F32),
            struct((rows, width), F32),
            *[struct((rows, TERMS * width + side(chunks, rows, BF16)), BF16)] * (pairs - 1),
            *[struct((chunks, LANES), F32)] * pairs,
        ),
        (got, terms, dots, sums),
    )
    sends, totals = refs[: pairs - 1], refs[pairs - 1 :]
    gots = [swap(s, "tp", kept(j + 1)) for j, s in enumerate(sends)]
    others = [
        swap(t, ("llm", "tp"), tp * g + kept(j)) for g in range(1, llm) for j, t in enumerate(totals)
    ]
    grad, total, *sends = run(
        part(combine_kernel, enc, pairs),
        (
            struct((rows, width), F32),
            struct((chunks, LANES), F32),
            *[struct((chunks + capacity * columns // LANES, LANES), F32)] * (enc - 1),
        ),
        (vis, bias, gain, inv_rms, kv, dots, own, totals[0], *gots, *others[::-1]),
        scratch=[pltpu.VMEM((rows, width), F32)],
    )
    gots = [swap(s, "enc", k + 1) for k, s in enumerate(sends)]
    (visual_grad,) = run(round_kernel, (struct((buckets, capacity, width), BF16),), (grad,))
    bias_grad, key_values = run(
        part(final_kernel, enc),
        (struct((chunks, LANES), F32), struct((buckets, capacity, columns), BF16)),
        (total, kv, *gots[::-1]),
    )
    return (key_values[None, None], visual_grad[None, None], bias_grad.reshape(width))


def solution(mesh):
    return jax.shard_map(
        per_device,
        mesh=mesh,
        in_specs=(
            P("enc", "llm", None, None, None),
            P("enc", "llm", None),
            P(),
            P(),
            P(None, "tp"),
            P("enc", "llm", None, None, "tp"),
        ),
        out_specs=(P("enc", "llm", None, None, "tp"), P("enc", "llm", None, None, "tp"), P("tp")),
        check_vma=False,
    )
```

```python
import functools

import jax
import jax.numpy as jnp
from jax import lax
from jax.experimental import pallas as pl
from jax.experimental.pallas import tpu as pltpu
from jax.sharding import PartitionSpec as P

LANES = 128
PIECES = 3
TERMS = 2
VMEM = pl.BlockSpec(memory_space=pltpu.VMEM)
HBM = pl.BlockSpec(memory_space=pltpu.HBM)
F32 = jnp.float32
BF16 = jnp.bfloat16


def swap(x, axis, k):
    n = lax.axis_size(axis)
    return lax.ppermute(x, axis, [(i, i ^ k) for i in range(n)])


def call(limit, kernel, outs, args, scratch=(), specs=None):
    return pl.pallas_call(
        kernel,
        out_shape=tuple(outs),
        in_specs=specs or [VMEM] * len(args),
        out_specs=tuple(VMEM for _ in outs),
        scratch_shapes=list(scratch),
        compiler_params=pltpu.CompilerParams(vmem_limit_bytes=limit),
    )(*args)


def first_kernel(*refs):
    token_ref = refs[-1]
    token_ref[...] = jnp.zeros(token_ref.shape, F32)


def project_kernel(vis_ref, bias_ref, gain_ref, weight_ref, _, projected_ref, inv_ref, rows_ref, normed_ref):
    buckets, capacity, features = vis_ref.shape
    for q in range(buckets):
        rows_ref[q * capacity : (q + 1) * capacity, :] = vis_ref[q].astype(F32) + bias_ref[...]
    inputs = rows_ref[...]
    mean = jnp.sum(inputs * inputs, axis=1, keepdims=True) / features
    inv_rms = lax.rsqrt(mean + 1e-06)
    normed_ref[...] = (inputs * inv_rms * gain_ref[...]).astype(BF16)
    inv_ref[...] = jnp.broadcast_to(inv_rms, inv_ref.shape)
    projected_ref[...] = jnp.dot(normed_ref[...], weight_ref[...], preferred_element_type=F32)


def kept(j):
    return 2 * j + (1 if j else 0)


def split(value, dtype):
    if dtype == F32:
        return [value]
    pieces = []
    for _ in range(PIECES):
        pieces.append(value.astype(dtype))
        value = value - pieces[-1].astype(F32)
    return pieces


def side(count, rows, dtype):
    return LANES * (1 + (1 if dtype == F32 else PIECES) * -(-count // rows))


def put_side(send_ref, start, dots, lines):
    rows, dtype = send_ref.shape[0], send_ref.dtype
    lane = lax.broadcasted_iota(jnp.int32, dots.shape, 1)
    block = jnp.zeros(dots.shape, F32)
    for i, piece in enumerate(split(dots, dtype)):
        block = jnp.where(lane == i, piece.astype(F32), block)
    blocks = [block.astype(dtype)]
    spare = -lines.shape[0] % rows
    if spare:
        lines = jnp.concatenate([lines, jnp.zeros((spare, LANES), F32)], axis=0)
    for piece in split(lines, dtype):
        blocks += [piece[i : i + rows] for i in range(0, piece.shape[0], rows)]
    for i, block in enumerate(blocks):
        send_ref[:, start + i * LANES : start + (i + 1) * LANES] = block


def get_dots(got_ref, start):
    return jnp.sum(got_ref[:, start : start + LANES].astype(F32), axis=1, keepdims=True)


def get_lines(got_ref, start, count):
    rows = got_ref.shape[0]
    each = -(-count // rows)
    blocks = [got_ref[:, i : i + LANES].astype(F32) for i in range(start + LANES, got_ref.shape[1], LANES)]
    total = None
    for i in range(0, len(blocks), each):
        piece = blocks[i] if each == 1 else jnp.concatenate(blocks[i : i + each], axis=0)
        total = piece if total is None else total + piece
    return total[:count]


def products(steps, tp, lhs, weight_ref, out_ref):
    width = weight_ref.shape[0] // tp
    place = lax.axis_index("tp")
    for j, k in enumerate(steps):
        cols = pl.ds(pl.multiple_of((place ^ k) * width, width), width)
        out_ref[:, j * width : (j + 1) * width] = lax.dot_general(
            lhs, weight_ref[cols, :], (((1,), (1,)), ((), ())), preferred_element_type=F32
        )


def row_sum(k, tp, term, vis_ref, bias_ref, gain_ref, inv_rms, dots):
    buckets, capacity, features = vis_ref.shape
    width = features // tp
    place = lax.axis_index("tp")
    cols = pl.ds(pl.multiple_of((place ^ k) * width, width), width)
    scale = inv_rms * inv_rms * dots * (1.0 / features)
    row = gain_ref[:, cols] * jnp.sum(inv_rms * term, axis=0, keepdims=True)
    for q in range(buckets):
        part = scale[q * capacity : (q + 1) * capacity]
        inputs = vis_ref[q, :, cols].astype(F32) + bias_ref[:, cols]
        row = row - jnp.sum(inputs * part, axis=0, keepdims=True)
    return row


def sent_kernel(enc, tp, counts_ref, projected_ref, weight_ref, vis_ref, bias_ref, gain_ref, inv_ref, *refs):
    cots = refs[:enc]
    kv_ref, dots_ref, lhs_ref, send_ref, sums_ref = refs[enc:]
    buckets, capacity, columns = kv_ref.shape
    me = lax.axis_index("enc")
    slot = lax.broadcasted_iota(jnp.int32, (capacity, columns), 0)
    blocks = [cot[me].astype(F32) for cot in cots]
    parts = []
    for q in range(buckets):
        block = blocks[0]
        for k in range(1, enc):
            block = jnp.where((me ^ k) == q, blocks[k], block)
        live = slot < counts_ref[:, q : q + 1]
        parts.append(jnp.where(live, block, 0.0))
        kv_ref[q] = jnp.where(live, projected_ref[q * capacity : (q + 1) * capacity, :], 0.0)
    masked = jnp.concatenate(parts, axis=0)
    lhs = masked.astype(BF16)
    lhs_ref[...] = lhs
    steps = [kept(j) ^ 1 for j in range(tp // 2)]
    products(steps, tp, lhs, weight_ref, send_ref)
    dots = jnp.sum(masked * projected_ref[...], axis=1, keepdims=True)
    dots_ref[...] = jnp.broadcast_to(dots, dots_ref.shape)
    width = vis_ref.shape[2] // tp
    chunks, half = width // LANES, tp // 2 * width
    inv_rms = inv_ref[:, :1]
    for j, k in enumerate(steps):
        term = send_ref[:, j * width : (j + 1) * width]
        row = row_sum(k, tp, term, vis_ref, bias_ref, gain_ref, inv_rms, dots)
        for i in range(chunks):
            sums_ref[j * chunks + i : j * chunks + i + 1, :] = row[:, i * LANES : (i + 1) * LANES]
    put_side(send_ref, half, dots_ref[...], sums_ref[...])


def kept_kernel(tp, lhs_ref, weight_ref, vis_ref, bias_ref, gain_ref, inv_ref, dots_ref, kept_ref, sums_ref):
    width = vis_ref.shape[2] // tp
    chunks = width // LANES
    steps = [kept(j) for j in range(tp // 2)]
    products(steps, tp, lhs_ref[...], weight_ref, kept_ref)
    for j, k in enumerate(steps):
        term = kept_ref[:, j * width : (j + 1) * width]
        row = row_sum(k, tp, term, vis_ref, bias_ref, gain_ref, inv_ref[:, :1], dots_ref[:, :1])
        for i in range(chunks):
            sums_ref[j * chunks + i : j * chunks + i + 1, :] = row[:, i * LANES : (i + 1) * LANES]


def fold_kernel(width, got_ref, kept_ref, dots_ref, sums_ref, all_ref, own_ref, *refs):
    pairs = kept_ref.shape[1] // width
    half, chunks = kept_ref.shape[1], width // LANES
    sends, totals = refs[: pairs - 1], refs[pairs - 1 :]
    dots = dots_ref[...] + get_dots(got_ref, half)
    all_ref[...] = dots
    sums = sums_ref[...] + get_lines(got_ref, half, pairs * chunks)
    for j in range(pairs):
        cols = slice(j * width, (j + 1) * width)
        term = kept_ref[:, cols] + got_ref[:, cols]
        lines = sums[j * chunks : (j + 1) * chunks]
        totals[j][...] = lines
        if j:
            for i in range(TERMS):
                piece = term.astype(BF16)
                sends[j - 1][:, i * width : (i + 1) * width] = piece
                term = term - piece.astype(F32)
            put_side(sends[j - 1], TERMS * width, dots, lines)
        else:
            own_ref[...] = term


def pack_kernel(enc, pairs, kv_ref, sum_ref, *refs):
    gots, refs = refs[: pairs - 1], refs[pairs - 1 :]
    sums, (total_ref, *sends) = refs[:-enc], refs[-enc:]
    chunks, capacity = sum_ref.shape[0], kv_ref.shape[1]
    me = lax.axis_index("enc")
    total = sum_ref[...]
    for got in sums:
        total = total + got[...]
    for got in gots:
        start = got.shape[1] - side(chunks, got.shape[0], BF16)
        total = total + get_lines(got, start, chunks)
    total_ref[...] = total
    for k in range(1, enc):
        sends[k - 1][:chunks, :] = total
        block = kv_ref[me ^ k]
        for j in range(block.shape[1] // LANES):
            at = chunks + j * capacity
            sends[k - 1][at : at + capacity, :] = block[:, j * LANES : (j + 1) * LANES]


def combine_kernel(vis_ref, bias_ref, gain_ref, inv_ref, dots_ref, own_ref, *refs):
    gots, (out_ref, token_ref) = refs[:-2], refs[-2:]
    buckets, capacity, features = vis_ref.shape
    width = own_ref.shape[1]
    place = lax.axis_index("tp")
    own = pl.ds(pl.multiple_of(place * width, width), width)
    grad_normed, row_dot = own_ref[...], dots_ref[:, :1]
    for got in gots:
        for i in range(TERMS):
            grad_normed = grad_normed + got[:, i * width : (i + 1) * width].astype(F32)
        row_dot = row_dot + get_dots(got, TERMS * width)
    inv_rms = inv_ref[:, :1]
    first = inv_rms * gain_ref[:, own] * grad_normed
    scale = inv_rms * inv_rms * row_dot * (1.0 / features)
    for q in range(buckets):
        rows = slice(q * capacity, (q + 1) * capacity)
        inputs = vis_ref[q, :, own].astype(F32) + bias_ref[:, own]
        out_ref[q] = (first[rows] - inputs * scale[rows]).astype(BF16)
    token_ref[...] = jnp.zeros(token_ref.shape, F32)


def final_kernel(enc, total_ref, kv_ref, _, *refs):
    gots, (sum_ref, out_ref) = refs[: enc - 1][::-1], refs[enc - 1 :]
    buckets, capacity, columns = kv_ref.shape
    chunks = total_ref.shape[0]
    me = lax.axis_index("enc")
    total = total_ref[...]
    for got in gots:
        total = total + got[:chunks, :]
    sum_ref[...] = total
    out_ref[me] = kv_ref[me].astype(BF16)
    for k in range(1, enc):
        for j in range(columns // LANES):
            at = chunks + j * capacity
            out_ref[me ^ k, :, j * LANES : (j + 1) * LANES] = gots[k - 1][
                at : at + capacity, :
            ].astype(BF16)


def per_device(visual, counts, merger_bias, norm_gain, kv_weight, kv_cotangent):
    buckets, capacity, features = visual.shape[2:]
    enc, llm, tp = (lax.axis_size(a) for a in ("enc", "llm", "tp"))
    width, columns, rows = features // tp, kv_weight.shape[1], buckets * capacity
    chunks, pairs = width // LANES, tp // 2
    half = pairs * width
    part = functools.partial
    struct = jax.ShapeDtypeStruct
    run = part(call, 2 * kv_weight.size * 2 + 16 * rows * features)

    vis, bias, gain, cot = visual[0, 0], merger_bias[None], norm_gain[None], kv_cotangent[0, 0]
    (token,) = run(
        first_kernel,
        (struct((8, LANES), F32),),
        [pltpu.with_memory_space_constraint(a, pltpu.HBM) for a in (kv_weight, vis, bias, gain)],
        specs=[HBM] * 4,
    )
    projected, inv_rms = run(
        project_kernel,
        (struct((rows, columns), F32), struct((rows, LANES), F32)),
        (vis, bias, gain, kv_weight, token),
        scratch=[pltpu.VMEM((rows, features), F32), pltpu.VMEM((rows, features), BF16)],
    )
    own_cot = cot
    cots = [own_cot] + [swap(cot, "enc", k) for k in range(1, enc)]
    kv, dots, lhs, send = run(
        part(sent_kernel, enc, tp),
        (
            struct((buckets, capacity, columns), F32),
            struct((rows, LANES), F32),
            struct((rows, columns), BF16),
            struct((rows, half + side(pairs * chunks, rows, F32)), F32),
        ),
        (counts[0], projected, kv_weight, vis, bias, gain, inv_rms, *cots),
        scratch=[pltpu.VMEM((pairs * chunks, LANES), F32)],
    )
    got = swap(send, "tp", 1)
    terms, sums = run(
        part(kept_kernel, tp),
        (struct((rows, half), F32), struct((pairs * chunks, LANES), F32)),
        (lhs, kv_weight, vis, bias, gain, inv_rms, dots),
    )
    dots, own, *refs = run(
        part(fold_kernel, width),
        (
            struct((rows, LANES), F32),
            struct((rows, width), F32),
            *[struct((rows, TERMS * width + side(chunks, rows, BF16)), BF16)] * (pairs - 1),
            *[struct((chunks, LANES), F32)] * pairs,
        ),
        (got, terms, dots, sums),
    )
    sends, totals = refs[: pairs - 1], refs[pairs - 1 :]
    gots = [swap(s, "tp", kept(j + 1)) for j, s in enumerate(sends)]
    others = [
        swap(t, ("llm", "tp"), tp * g + kept(j)) for g in range(1, llm) for j, t in enumerate(totals)
    ]
    total, *sends = run(
        part(pack_kernel, enc, pairs),
        (
            struct((chunks, LANES), F32),
            *[struct((chunks + capacity * columns // LANES, LANES), F32)] * (enc - 1),
        ),
        (kv, totals[0], *gots, *others[::-1]),
    )
    visual_grad, token = run(
        combine_kernel,
        (struct((buckets, capacity, width), BF16), struct((8, LANES), F32)),
        (vis, bias, gain, inv_rms, dots, own, *gots),
    )
    gots = [swap(s, "enc", k + 1) for k, s in enumerate(sends)]
    bias_grad, key_values = run(
        part(final_kernel, enc),
        (struct((chunks, LANES), F32), struct((buckets, capacity, columns), BF16)),
        (total, kv, token, *gots[::-1]),
    )
    return (key_values[None, None], visual_grad[None, None], bias_grad.reshape(width))


def solution(mesh):
    return jax.shard_map(
        per_device,
        mesh=mesh,
        in_specs=(
            P("enc", "llm", None, None, None),
            P("enc", "llm", None),
            P(),
            P(),
            P(None, "tp"),
            P("enc", "llm", None, None, "tp"),
        ),
        out_specs=(P("enc", "llm", None, None, "tp"), P("enc", "llm", None, None, "tp"), P("tp")),
        check_vma=False,
    )
```

```python
import functools

import jax
import jax.numpy as jnp
from jax import lax
from jax.experimental import pallas as pl
from jax.experimental.pallas import tpu as pltpu
from jax.sharding import PartitionSpec as P

LANES = 128
PIECES = 3
TERMS = 2
STEPS = 8
TURNED = 2
VMEM = pl.BlockSpec(memory_space=pltpu.VMEM)
HBM = pl.BlockSpec(memory_space=pltpu.HBM)
F32 = jnp.float32
BF16 = jnp.bfloat16


def swap(x, axis, k):
    n = lax.axis_size(axis)
    return lax.ppermute(x, axis, [(i, i ^ k) for i in range(n)])


def call(limit, kernel, outs, args, scratch=(), specs=None):
    return pl.pallas_call(
        kernel,
        out_shape=tuple(outs),
        in_specs=specs or [VMEM] * len(args),
        out_specs=tuple(VMEM for _ in outs),
        scratch_shapes=list(scratch),
        compiler_params=pltpu.CompilerParams(vmem_limit_bytes=limit),
    )(*args)


def first_kernel(*refs):
    token_ref = refs[-1]
    token_ref[...] = jnp.zeros(token_ref.shape, F32)


def project_kernel(
    tp, vis_ref, bias_ref, gain_ref, weight_ref, _, projected_ref, inv_ref, turned_ref, rows_ref, normed_ref
):
    buckets, capacity, features = vis_ref.shape
    for q in range(buckets):
        rows_ref[q * capacity : (q + 1) * capacity, :] = vis_ref[q].astype(F32) + bias_ref[...]
    inputs = rows_ref[...]
    mean = jnp.sum(inputs * inputs, axis=1, keepdims=True) / features
    inv_rms = lax.rsqrt(mean + 1e-06)
    normed_ref[...] = (inputs * inv_rms * gain_ref[...]).astype(BF16)
    inv_ref[...] = jnp.broadcast_to(inv_rms, inv_ref.shape)
    count, width = turned_ref.shape[0], features // tp
    place, step = lax.axis_index("tp"), features // STEPS
    projected = jnp.zeros(projected_ref.shape, F32)
    for i in range(STEPS):
        part = slice(i * step, (i + 1) * step)
        projected = projected + jnp.dot(
            normed_ref[:, part], weight_ref[part, :], preferred_element_type=F32
        )
        size = width // STEPS
        for j in range(count):
            start = pl.multiple_of((place ^ kept(j) ^ 1) * width, width)
            block = weight_ref[pl.ds(start + i * size, size), :]
            turned_ref[j, :, i * size : (i + 1) * size] = block.T
    projected_ref[...] = projected


def kept(j):
    return 2 * j + (1 if j else 0)


def split(value, dtype):
    if dtype == F32:
        return [value]
    pieces = []
    for _ in range(PIECES):
        pieces.append(value.astype(dtype))
        value = value - pieces[-1].astype(F32)
    return pieces


def side(count, rows, dtype):
    return LANES * (1 + (1 if dtype == F32 else PIECES) * -(-count // rows))


def put_side(send_ref, start, dots, lines):
    rows, dtype = send_ref.shape[0], send_ref.dtype
    lane = lax.broadcasted_iota(jnp.int32, dots.shape, 1)
    block = jnp.zeros(dots.shape, F32)
    for i, piece in enumerate(split(dots, dtype)):
        block = jnp.where(lane == i, piece.astype(F32), block)
    blocks = [block.astype(dtype)]
    spare = -lines.shape[0] % rows
    if spare:
        lines = jnp.concatenate([lines, jnp.zeros((spare, LANES), F32)], axis=0)
    for piece in split(lines, dtype):
        blocks += [piece[i : i + rows] for i in range(0, piece.shape[0], rows)]
    for i, block in enumerate(blocks):
        send_ref[:, start + i * LANES : start + (i + 1) * LANES] = block


def get_dots(got_ref, start):
    return jnp.sum(got_ref[:, start : start + LANES].astype(F32), axis=1, keepdims=True)


def get_lines(got_ref, start, count):
    rows = got_ref.shape[0]
    each = -(-count // rows)
    blocks = [got_ref[:, i : i + LANES].astype(F32) for i in range(start + LANES, got_ref.shape[1], LANES)]
    total = None
    for i in range(0, len(blocks), each):
        piece = blocks[i] if each == 1 else jnp.concatenate(blocks[i : i + each], axis=0)
        total = piece if total is None else total + piece
    return total[:count]


def products(steps, tp, lhs, weight_ref, out_ref, first=0):
    width = weight_ref.shape[0] // tp
    place = lax.axis_index("tp")
    for j, k in enumerate(steps, first):
        cols = pl.ds(pl.multiple_of((place ^ k) * width, width), width)
        out_ref[:, j * width : (j + 1) * width] = lax.dot_general(
            lhs, weight_ref[cols, :], (((1,), (1,)), ((), ())), preferred_element_type=F32
        )


def row_sum(k, tp, term, vis_ref, bias_ref, gain_ref, inv_rms, dots):
    buckets, capacity, features = vis_ref.shape
    width = features // tp
    place = lax.axis_index("tp")
    cols = pl.ds(pl.multiple_of((place ^ k) * width, width), width)
    scale = inv_rms * inv_rms * dots * (1.0 / features)
    row = gain_ref[:, cols] * jnp.sum(inv_rms * term, axis=0, keepdims=True)
    for q in range(buckets):
        part = scale[q * capacity : (q + 1) * capacity]
        inputs = vis_ref[q, :, cols].astype(F32) + bias_ref[:, cols]
        row = row - jnp.sum(inputs * part, axis=0, keepdims=True)
    return row


def sent_kernel(enc, tp, counts_ref, projected_ref, turned_ref, weight_ref, vis_ref, bias_ref, gain_ref, inv_ref, *refs):
    cots = refs[:enc]
    kv_ref, dots_ref, lhs_ref, send_ref, sums_ref = refs[enc:]
    buckets, capacity, columns = kv_ref.shape
    me = lax.axis_index("enc")
    slot = lax.broadcasted_iota(jnp.int32, (capacity, columns), 0)
    blocks = [cot[me].astype(F32) for cot in cots]
    parts = []
    for q in range(buckets):
        block = blocks[0]
        for k in range(1, enc):
            block = jnp.where((me ^ k) == q, blocks[k], block)
        live = slot < counts_ref[:, q : q + 1]
        parts.append(jnp.where(live, block, 0.0))
        kv_ref[q] = jnp.where(live, projected_ref[q * capacity : (q + 1) * capacity, :], 0.0)
    masked = jnp.concatenate(parts, axis=0)
    lhs = masked.astype(BF16)
    lhs_ref[...] = lhs
    steps = [kept(j) ^ 1 for j in range(tp // 2)]
    count, _, width = turned_ref.shape
    for j in range(count):
        send_ref[:, j * width : (j + 1) * width] = jnp.dot(
            lhs, turned_ref[j], preferred_element_type=F32
        )
    products(steps[count:], tp, lhs, weight_ref, send_ref, count)
    dots = jnp.sum(masked * projected_ref[...], axis=1, keepdims=True)
    dots_ref[...] = jnp.broadcast_to(dots, dots_ref.shape)
    width = vis_ref.shape[2] // tp
    chunks, half = width // LANES, tp // 2 * width
    inv_rms = inv_ref[:, :1]
    for j, k in enumerate(steps):
        term = send_ref[:, j * width : (j + 1) * width]
        row = row_sum(k, tp, term, vis_ref, bias_ref, gain_ref, inv_rms, dots)
        for i in range(chunks):
            sums_ref[j * chunks + i : j * chunks + i + 1, :] = row[:, i * LANES : (i + 1) * LANES]
    put_side(send_ref, half, dots_ref[...], sums_ref[...])


def kept_kernel(tp, lhs_ref, weight_ref, vis_ref, bias_ref, gain_ref, inv_ref, dots_ref, kept_ref, sums_ref):
    width = vis_ref.shape[2] // tp
    chunks = width // LANES
    steps = [kept(j) for j in range(tp // 2)]
    products(steps, tp, lhs_ref[...], weight_ref, kept_ref)
    for j, k in enumerate(steps):
        term = kept_ref[:, j * width : (j + 1) * width]
        row = row_sum(k, tp, term, vis_ref, bias_ref, gain_ref, inv_ref[:, :1], dots_ref[:, :1])
        for i in range(chunks):
            sums_ref[j * chunks + i : j * chunks + i + 1, :] = row[:, i * LANES : (i + 1) * LANES]


def fold_kernel(width, got_ref, kept_ref, dots_ref, sums_ref, all_ref, own_ref, *refs):
    pairs = kept_ref.shape[1] // width
    half, chunks = kept_ref.shape[1], width // LANES
    sends, totals = refs[: pairs - 1], refs[pairs - 1 :]
    dots = dots_ref[...] + get_dots(got_ref, half)
    all_ref[...] = dots
    sums = sums_ref[...] + get_lines(got_ref, half, pairs * chunks)
    for j in range(pairs):
        cols = slice(j * width, (j + 1) * width)
        term = kept_ref[:, cols] + got_ref[:, cols]
        lines = sums[j * chunks : (j + 1) * chunks]
        totals[j][...] = lines
        if j:
            for i in range(TERMS):
                piece = term.astype(BF16)
                sends[j - 1][:, i * width : (i + 1) * width] = piece
                term = term - piece.astype(F32)
            put_side(sends[j - 1], TERMS * width, dots, lines)
        else:
            own_ref[...] = term


def pack_kernel(enc, pairs, kv_ref, sum_ref, *refs):
    gots, refs = refs[: pairs - 1], refs[pairs - 1 :]
    sums, (total_ref, *sends) = refs[:-enc], refs[-enc:]
    chunks, capacity = sum_ref.shape[0], kv_ref.shape[1]
    me = lax.axis_index("enc")
    total = sum_ref[...]
    for got in sums:
        total = total + got[...]
    for got in gots:
        start = got.shape[1] - side(chunks, got.shape[0], BF16)
        total = total + get_lines(got, start, chunks)
    total_ref[...] = total
    for k in range(1, enc):
        sends[k - 1][:chunks, :] = total
        block = kv_ref[me ^ k]
        for j in range(block.shape[1] // LANES):
            at = chunks + j * capacity
            sends[k - 1][at : at + capacity, :] = block[:, j * LANES : (j + 1) * LANES]


def combine_kernel(vis_ref, bias_ref, gain_ref, inv_ref, dots_ref, own_ref, *refs):
    gots, (out_ref, token_ref) = refs[:-2], refs[-2:]
    buckets, capacity, features = vis_ref.shape
    width = own_ref.shape[1]
    place = lax.axis_index("tp")
    own = pl.ds(pl.multiple_of(place * width, width), width)
    grad_normed, row_dot = own_ref[...], dots_ref[:, :1]
    for got in gots:
        for i in range(TERMS):
            grad_normed = grad_normed + got[:, i * width : (i + 1) * width].astype(F32)
        row_dot = row_dot + get_dots(got, TERMS * width)
    inv_rms = inv_ref[:, :1]
    first = inv_rms * gain_ref[:, own] * grad_normed
    scale = inv_rms * inv_rms * row_dot * (1.0 / features)
    for q in range(buckets):
        rows = slice(q * capacity, (q + 1) * capacity)
        inputs = vis_ref[q, :, own].astype(F32) + bias_ref[:, own]
        out_ref[q] = (first[rows] - inputs * scale[rows]).astype(BF16)
    token_ref[...] = jnp.zeros(token_ref.shape, F32)


def final_kernel(enc, total_ref, kv_ref, _, *refs):
    gots, (sum_ref, out_ref) = refs[: enc - 1][::-1], refs[enc - 1 :]
    buckets, capacity, columns = kv_ref.shape
    chunks = total_ref.shape[0]
    me = lax.axis_index("enc")
    total = total_ref[...]
    for got in gots:
        total = total + got[:chunks, :]
    sum_ref[...] = total
    out_ref[me] = kv_ref[me].astype(BF16)
    for k in range(1, enc):
        for j in range(columns // LANES):
            at = chunks + j * capacity
            out_ref[me ^ k, :, j * LANES : (j + 1) * LANES] = gots[k - 1][
                at : at + capacity, :
            ].astype(BF16)


def per_device(visual, counts, merger_bias, norm_gain, kv_weight, kv_cotangent):
    buckets, capacity, features = visual.shape[2:]
    enc, llm, tp = (lax.axis_size(a) for a in ("enc", "llm", "tp"))
    width, columns, rows = features // tp, kv_weight.shape[1], buckets * capacity
    chunks, pairs = width // LANES, tp // 2
    half = pairs * width
    part = functools.partial
    struct = jax.ShapeDtypeStruct
    run = part(call, 2 * kv_weight.size * 2 + 16 * rows * features)

    vis, bias, gain, cot = visual[0, 0], merger_bias[None], norm_gain[None], kv_cotangent[0, 0]
    (token,) = run(
        first_kernel,
        (struct((8, LANES), F32),),
        [pltpu.with_memory_space_constraint(a, pltpu.HBM) for a in (kv_weight, vis, bias, gain)],
        specs=[HBM] * 4,
    )
    projected, inv_rms, turned = run(
        part(project_kernel, tp),
        (
            struct((rows, columns), F32),
            struct((rows, LANES), F32),
            struct((min(TURNED, pairs), columns, width), BF16),
        ),
        (vis, bias, gain, kv_weight, token),
        scratch=[pltpu.VMEM((rows, features), F32), pltpu.VMEM((rows, features), BF16)],
    )
    own_cot = cot
    cots = [own_cot] + [swap(cot, "enc", k) for k in range(1, enc)]
    kv, dots, lhs, send = run(
        part(sent_kernel, enc, tp),
        (
            struct((buckets, capacity, columns), F32),
            struct((rows, LANES), F32),
            struct((rows, columns), BF16),
            struct((rows, half + side(pairs * chunks, rows, F32)), F32),
        ),
        (counts[0], projected, turned, kv_weight, vis, bias, gain, inv_rms, *cots),
        scratch=[pltpu.VMEM((pairs * chunks, LANES), F32)],
    )
    got = swap(send, "tp", 1)
    terms, sums = run(
        part(kept_kernel, tp),
        (struct((rows, half), F32), struct((pairs * chunks, LANES), F32)),
        (lhs, kv_weight, vis, bias, gain, inv_rms, dots),
    )
    dots, own, *refs = run(
        part(fold_kernel, width),
        (
            struct((rows, LANES), F32),
            struct((rows, width), F32),
            *[struct((rows, TERMS * width + side(chunks, rows, BF16)), BF16)] * (pairs - 1),
            *[struct((chunks, LANES), F32)] * pairs,
        ),
        (got, terms, dots, sums),
    )
    sends, totals = refs[: pairs - 1], refs[pairs - 1 :]
    gots = [swap(s, "tp", kept(j + 1)) for j, s in enumerate(sends)]
    others = [
        swap(t, ("llm", "tp"), tp * g + kept(j)) for g in range(1, llm) for j, t in enumerate(totals)
    ]
    total, *sends = run(
        part(pack_kernel, enc, pairs),
        (
            struct((chunks, LANES), F32),
            *[struct((chunks + capacity * columns // LANES, LANES), F32)] * (enc - 1),
        ),
        (kv, totals[0], *gots, *others[::-1]),
    )
    visual_grad, token = run(
        combine_kernel,
        (struct((buckets, capacity, width), BF16), struct((8, LANES), F32)),
        (vis, bias, gain, inv_rms, dots, own, *gots),
    )
    gots = [swap(s, "enc", k + 1) for k, s in enumerate(sends)]
    bias_grad, key_values = run(
        part(final_kernel, enc),
        (struct((chunks, LANES), F32), struct((buckets, capacity, columns), BF16)),
        (total, kv, token, *gots[::-1]),
    )
    return (key_values[None, None], visual_grad[None, None], bias_grad.reshape(width))


def solution(mesh):
    return jax.shard_map(
        per_device,
        mesh=mesh,
        in_specs=(
            P("enc", "llm", None, None, None),
            P("enc", "llm", None),
            P(),
            P(),
            P(None, "tp"),
            P("enc", "llm", None, None, "tp"),
        ),
        out_specs=(P("enc", "llm", None, None, "tp"), P("enc", "llm", None, None, "tp"), P("tp")),
        check_vma=False,
    )
```

```python
import functools

import jax
import jax.numpy as jnp
from jax import lax
from jax.experimental import pallas as pl
from jax.experimental.pallas import tpu as pltpu
from jax.sharding import PartitionSpec as P

LANES = 128
PIECES = 3
TERMS = 2
STEPS = 8
TURNED = 2
VMEM = pl.BlockSpec(memory_space=pltpu.VMEM)
HBM = pl.BlockSpec(memory_space=pltpu.HBM)
F32 = jnp.float32
BF16 = jnp.bfloat16


def swap(x, axis, k):
    n = lax.axis_size(axis)
    return lax.ppermute(x, axis, [(i, i ^ k) for i in range(n)])


def call(limit, kernel, outs, args, scratch=(), specs=None):
    return pl.pallas_call(
        kernel,
        out_shape=tuple(outs),
        in_specs=specs or [VMEM] * len(args),
        out_specs=tuple(VMEM for _ in outs),
        scratch_shapes=list(scratch),
        compiler_params=pltpu.CompilerParams(vmem_limit_bytes=limit),
    )(*args)


def first_kernel(*refs):
    token_ref = refs[-1]
    token_ref[...] = jnp.zeros(token_ref.shape, F32)


def project_kernel(
    tp, vis_ref, bias_ref, gain_ref, weight_ref, _, projected_ref, inv_ref, turned_ref, rows_ref, normed_ref
):
    buckets, capacity, features = vis_ref.shape
    for q in range(buckets):
        rows_ref[q * capacity : (q + 1) * capacity, :] = vis_ref[q].astype(F32) + bias_ref[...]
    inputs = rows_ref[...]
    mean = jnp.sum(inputs * inputs, axis=1, keepdims=True) / features
    inv_rms = lax.rsqrt(mean + 1e-06)
    normed_ref[...] = (inputs * inv_rms * gain_ref[...]).astype(BF16)
    inv_ref[...] = jnp.broadcast_to(inv_rms, inv_ref.shape)
    count, width = turned_ref.shape[0], features // tp
    place, step = lax.axis_index("tp"), features // STEPS
    projected = jnp.zeros(projected_ref.shape, F32)
    for i in range(STEPS):
        part = slice(i * step, (i + 1) * step)
        projected = projected + jnp.dot(
            normed_ref[:, part], weight_ref[part, :], preferred_element_type=F32
        )
        size = width // STEPS
        for j in range(count):
            start = pl.multiple_of((place ^ kept(j) ^ 1) * width, width)
            block = weight_ref[pl.ds(start + i * size, size), :]
            turned_ref[j, :, i * size : (i + 1) * size] = block.T
    projected_ref[...] = projected


def kept(j):
    return 2 * j + (1 if j else 0)


def split(value, dtype):
    if dtype == F32:
        return [value]
    pieces = []
    for _ in range(PIECES):
        pieces.append(value.astype(dtype))
        value = value - pieces[-1].astype(F32)
    return pieces


def side(count, rows, dtype):
    return LANES * (1 + (1 if dtype == F32 else PIECES) * -(-count // rows))


def put_side(send_ref, start, dots, lines):
    rows, dtype = send_ref.shape[0], send_ref.dtype
    lane = lax.broadcasted_iota(jnp.int32, dots.shape, 1)
    block = jnp.zeros(dots.shape, F32)
    for i, piece in enumerate(split(dots, dtype)):
        block = jnp.where(lane == i, piece.astype(F32), block)
    blocks = [block.astype(dtype)]
    spare = -lines.shape[0] % rows
    if spare:
        lines = jnp.concatenate([lines, jnp.zeros((spare, LANES), F32)], axis=0)
    for piece in split(lines, dtype):
        blocks += [piece[i : i + rows] for i in range(0, piece.shape[0], rows)]
    for i, block in enumerate(blocks):
        send_ref[:, start + i * LANES : start + (i + 1) * LANES] = block


def get_dots(got_ref, start):
    return jnp.sum(got_ref[:, start : start + LANES].astype(F32), axis=1, keepdims=True)


def get_lines(got_ref, start, count):
    rows = got_ref.shape[0]
    each = -(-count // rows)
    blocks = [got_ref[:, i : i + LANES].astype(F32) for i in range(start + LANES, got_ref.shape[1], LANES)]
    total = None
    for i in range(0, len(blocks), each):
        piece = blocks[i] if each == 1 else jnp.concatenate(blocks[i : i + each], axis=0)
        total = piece if total is None else total + piece
    return total[:count]


def products(steps, tp, lhs, weight_ref, out_ref, first=0):
    width = weight_ref.shape[0] // tp
    place = lax.axis_index("tp")
    for j, k in enumerate(steps, first):
        cols = pl.ds(pl.multiple_of((place ^ k) * width, width), width)
        out_ref[:, j * width : (j + 1) * width] = lax.dot_general(
            lhs, weight_ref[cols, :], (((1,), (1,)), ((), ())), preferred_element_type=F32
        )


def row_sum(k, tp, term, rows_ref, gain_ref, inv_rms, dots):
    features = rows_ref.shape[1]
    width = features // tp
    place = lax.axis_index("tp")
    cols = pl.ds(pl.multiple_of((place ^ k) * width, width), width)
    scale = inv_rms * inv_rms * dots * (1.0 / features)
    row = gain_ref[:, cols] * jnp.sum(inv_rms * term, axis=0, keepdims=True)
    return row - jnp.sum(rows_ref[:, cols] * scale, axis=0, keepdims=True)


def sent_kernel(enc, tp, counts_ref, projected_ref, turned_ref, weight_ref, rows_ref, gain_ref, inv_ref, *refs):
    cots = refs[:enc]
    kv_ref, dots_ref, lhs_ref, send_ref, sums_ref = refs[enc:]
    buckets, capacity, columns = kv_ref.shape
    me = lax.axis_index("enc")
    slot = lax.broadcasted_iota(jnp.int32, (capacity, columns), 0)
    blocks = [cot[me].astype(F32) for cot in cots]
    parts = []
    for q in range(buckets):
        block = blocks[0]
        for k in range(1, enc):
            block = jnp.where((me ^ k) == q, blocks[k], block)
        live = slot < counts_ref[:, q : q + 1]
        parts.append(jnp.where(live, block, 0.0))
        kv_ref[q] = jnp.where(live, projected_ref[q * capacity : (q + 1) * capacity, :], 0.0)
    masked = jnp.concatenate(parts, axis=0)
    lhs = masked.astype(BF16)
    lhs_ref[...] = lhs
    steps = [kept(j) ^ 1 for j in range(tp // 2)]
    count, _, width = turned_ref.shape
    for j in range(count):
        send_ref[:, j * width : (j + 1) * width] = jnp.dot(
            lhs, turned_ref[j], preferred_element_type=F32
        )
    products(steps[count:], tp, lhs, weight_ref, send_ref, count)
    dots = jnp.sum(masked * projected_ref[...], axis=1, keepdims=True)
    dots_ref[...] = jnp.broadcast_to(dots, dots_ref.shape)
    width = rows_ref.shape[1] // tp
    chunks, half = width // LANES, tp // 2 * width
    inv_rms = inv_ref[:, :1]
    for j, k in enumerate(steps):
        term = send_ref[:, j * width : (j + 1) * width]
        row = row_sum(k, tp, term, rows_ref, gain_ref, inv_rms, dots)
        for i in range(chunks):
            sums_ref[j * chunks + i : j * chunks + i + 1, :] = row[:, i * LANES : (i + 1) * LANES]
    put_side(send_ref, half, dots_ref[...], sums_ref[...])


def kept_kernel(tp, lhs_ref, weight_ref, rows_ref, gain_ref, inv_ref, dots_ref, kept_ref, sums_ref):
    width = rows_ref.shape[1] // tp
    chunks = width // LANES
    steps = [kept(j) for j in range(tp // 2)]
    products(steps, tp, lhs_ref[...], weight_ref, kept_ref)
    for j, k in enumerate(steps):
        term = kept_ref[:, j * width : (j + 1) * width]
        row = row_sum(k, tp, term, rows_ref, gain_ref, inv_ref[:, :1], dots_ref[:, :1])
        for i in range(chunks):
            sums_ref[j * chunks + i : j * chunks + i + 1, :] = row[:, i * LANES : (i + 1) * LANES]


def fold_kernel(width, got_ref, kept_ref, dots_ref, sums_ref, all_ref, own_ref, *refs):
    pairs = kept_ref.shape[1] // width
    half, chunks = kept_ref.shape[1], width // LANES
    sends, totals = refs[: pairs - 1], refs[pairs - 1 :]
    dots = dots_ref[...] + get_dots(got_ref, half)
    all_ref[...] = dots
    sums = sums_ref[...] + get_lines(got_ref, half, pairs * chunks)
    for j in range(pairs):
        cols = slice(j * width, (j + 1) * width)
        term = kept_ref[:, cols] + got_ref[:, cols]
        lines = sums[j * chunks : (j + 1) * chunks]
        totals[j][...] = lines
        if j:
            for i in range(TERMS):
                piece = term.astype(BF16)
                sends[j - 1][:, i * width : (i + 1) * width] = piece
                term = term - piece.astype(F32)
            put_side(sends[j - 1], TERMS * width, dots, lines)
        else:
            own_ref[...] = term


def pack_kernel(enc, pairs, kv_ref, sum_ref, *refs):
    gots, refs = refs[: pairs - 1], refs[pairs - 1 :]
    sums, (total_ref, *sends) = refs[:-enc], refs[-enc:]
    chunks, capacity = sum_ref.shape[0], kv_ref.shape[1]
    me = lax.axis_index("enc")
    total = sum_ref[...]
    for got in sums:
        total = total + got[...]
    for got in gots:
        start = got.shape[1] - side(chunks, got.shape[0], BF16)
        total = total + get_lines(got, start, chunks)
    total_ref[...] = total
    for k in range(1, enc):
        sends[k - 1][:chunks, :] = total
        block = kv_ref[me ^ k]
        for j in range(block.shape[1] // LANES):
            at = chunks + j * capacity
            sends[k - 1][at : at + capacity, :] = block[:, j * LANES : (j + 1) * LANES]


def combine_kernel(rows_ref, gain_ref, inv_ref, dots_ref, own_ref, *refs):
    gots, (out_ref, token_ref) = refs[:-2], refs[-2:]
    buckets, capacity, width = out_ref.shape
    features = rows_ref.shape[1]
    place = lax.axis_index("tp")
    own = pl.ds(pl.multiple_of(place * width, width), width)
    grad_normed, row_dot = own_ref[...], dots_ref[:, :1]
    for got in gots:
        for i in range(TERMS):
            grad_normed = grad_normed + got[:, i * width : (i + 1) * width].astype(F32)
        row_dot = row_dot + get_dots(got, TERMS * width)
    inv_rms = inv_ref[:, :1]
    first = inv_rms * gain_ref[:, own] * grad_normed
    scale = inv_rms * inv_rms * row_dot * (1.0 / features)
    grad_rows = first - rows_ref[:, own] * scale
    for q in range(buckets):
        out_ref[q] = grad_rows[q * capacity : (q + 1) * capacity].astype(BF16)
    token_ref[...] = jnp.zeros(token_ref.shape, F32)


def final_kernel(enc, total_ref, kv_ref, _, *refs):
    gots, (sum_ref, out_ref) = refs[: enc - 1][::-1], refs[enc - 1 :]
    buckets, capacity, columns = kv_ref.shape
    chunks = total_ref.shape[0]
    me = lax.axis_index("enc")
    total = total_ref[...]
    for got in gots:
        total = total + got[:chunks, :]
    sum_ref[...] = total
    out_ref[me] = kv_ref[me].astype(BF16)
    for k in range(1, enc):
        for j in range(columns // LANES):
            at = chunks + j * capacity
            out_ref[me ^ k, :, j * LANES : (j + 1) * LANES] = gots[k - 1][
                at : at + capacity, :
            ].astype(BF16)


def per_device(visual, counts, merger_bias, norm_gain, kv_weight, kv_cotangent):
    buckets, capacity, features = visual.shape[2:]
    enc, llm, tp = (lax.axis_size(a) for a in ("enc", "llm", "tp"))
    width, columns, rows = features // tp, kv_weight.shape[1], buckets * capacity
    chunks, pairs = width // LANES, tp // 2
    half = pairs * width
    part = functools.partial
    struct = jax.ShapeDtypeStruct
    run = part(call, 2 * kv_weight.size * 2 + 16 * rows * features)

    vis, bias, gain, cot = visual[0, 0], merger_bias[None], norm_gain[None], kv_cotangent[0, 0]
    (token,) = run(
        first_kernel,
        (struct((8, LANES), F32),),
        [pltpu.with_memory_space_constraint(a, pltpu.HBM) for a in (kv_weight, vis, bias, gain)],
        specs=[HBM] * 4,
    )
    projected, inv_rms, turned, inputs = run(
        part(project_kernel, tp),
        (
            struct((rows, columns), F32),
            struct((rows, LANES), F32),
            struct((min(TURNED, pairs), columns, width), BF16),
            struct((rows, features), F32),
        ),
        (vis, bias, gain, kv_weight, token),
        scratch=[pltpu.VMEM((rows, features), BF16)],
    )
    own_cot = cot
    cots = [own_cot] + [swap(cot, "enc", k) for k in range(1, enc)]
    kv, dots, lhs, send = run(
        part(sent_kernel, enc, tp),
        (
            struct((buckets, capacity, columns), F32),
            struct((rows, LANES), F32),
            struct((rows, columns), BF16),
            struct((rows, half + side(pairs * chunks, rows, F32)), F32),
        ),
        (counts[0], projected, turned, kv_weight, inputs, gain, inv_rms, *cots),
        scratch=[pltpu.VMEM((pairs * chunks, LANES), F32)],
    )
    got = swap(send, "tp", 1)
    terms, sums = run(
        part(kept_kernel, tp),
        (struct((rows, half), F32), struct((pairs * chunks, LANES), F32)),
        (lhs, kv_weight, inputs, gain, inv_rms, dots),
    )
    dots, own, *refs = run(
        part(fold_kernel, width),
        (
            struct((rows, LANES), F32),
            struct((rows, width), F32),
            *[struct((rows, TERMS * width + side(chunks, rows, BF16)), BF16)] * (pairs - 1),
            *[struct((chunks, LANES), F32)] * pairs,
        ),
        (got, terms, dots, sums),
    )
    sends, totals = refs[: pairs - 1], refs[pairs - 1 :]
    gots = [swap(s, "tp", kept(j + 1)) for j, s in enumerate(sends)]
    others = [
        swap(t, ("llm", "tp"), tp * g + kept(j)) for g in range(1, llm) for j, t in enumerate(totals)
    ]
    total, *sends = run(
        part(pack_kernel, enc, pairs),
        (
            struct((chunks, LANES), F32),
            *[struct((chunks + capacity * columns // LANES, LANES), F32)] * (enc - 1),
        ),
        (kv, totals[0], *gots, *others[::-1]),
    )
    visual_grad, token = run(
        combine_kernel,
        (struct((buckets, capacity, width), BF16), struct((8, LANES), F32)),
        (inputs, gain, inv_rms, dots, own, *gots),
    )
    gots = [swap(s, "enc", k + 1) for k, s in enumerate(sends)]
    bias_grad, key_values = run(
        part(final_kernel, enc),
        (struct((chunks, LANES), F32), struct((buckets, capacity, columns), BF16)),
        (total, kv, token, *gots[::-1]),
    )
    return (key_values[None, None], visual_grad[None, None], bias_grad.reshape(width))


def solution(mesh):
    return jax.shard_map(
        per_device,
        mesh=mesh,
        in_specs=(
            P("enc", "llm", None, None, None),
            P("enc", "llm", None),
            P(),
            P(),
            P(None, "tp"),
            P("enc", "llm", None, None, "tp"),
        ),
        out_specs=(P("enc", "llm", None, None, "tp"), P("enc", "llm", None, None, "tp"), P("tp")),
        check_vma=False,
    )
```

```python
import functools

import jax
import jax.numpy as jnp
from jax import lax
from jax.experimental import pallas as pl
from jax.experimental.pallas import tpu as pltpu
from jax.sharding import PartitionSpec as P

LANES = 128
PIECES = 3
TERMS = 2
STEPS = 4
TURNED = 2
VMEM = pl.BlockSpec(memory_space=pltpu.VMEM)
HBM = pl.BlockSpec(memory_space=pltpu.HBM)
F32 = jnp.float32
BF16 = jnp.bfloat16


def swap(x, axis, k):
    n = lax.axis_size(axis)
    return lax.ppermute(x, axis, [(i, i ^ k) for i in range(n)])


def call(limit, kernel, outs, args, scratch=(), specs=None):
    return pl.pallas_call(
        kernel,
        out_shape=tuple(outs),
        in_specs=specs or [VMEM] * len(args),
        out_specs=tuple(VMEM for _ in outs),
        scratch_shapes=list(scratch),
        compiler_params=pltpu.CompilerParams(vmem_limit_bytes=limit),
    )(*args)


def first_kernel(*refs):
    token_ref = refs[-1]
    token_ref[...] = jnp.zeros(token_ref.shape, F32)


def project_kernel(
    tp, vis_ref, bias_ref, gain_ref, weight_ref, _, projected_ref, inv_ref, turned_ref, rows_ref, normed_ref
):
    buckets, capacity, features = vis_ref.shape
    for q in range(buckets):
        rows_ref[q * capacity : (q + 1) * capacity, :] = vis_ref[q].astype(F32) + bias_ref[...]
    inputs = rows_ref[...]
    mean = jnp.sum(inputs * inputs, axis=1, keepdims=True) / features
    inv_rms = lax.rsqrt(mean + 1e-06)
    normed_ref[...] = (inputs * inv_rms * gain_ref[...]).astype(BF16)
    inv_ref[...] = jnp.broadcast_to(inv_rms, inv_ref.shape)
    count, width = turned_ref.shape[0], features // tp
    place, step = lax.axis_index("tp"), features // STEPS
    projected = jnp.zeros(projected_ref.shape, F32)
    for i in range(STEPS):
        part = slice(i * step, (i + 1) * step)
        projected = projected + jnp.dot(
            normed_ref[:, part], weight_ref[part, :], preferred_element_type=F32
        )
        size = width // STEPS
        for j in range(count):
            start = pl.multiple_of((place ^ kept(j) ^ 1) * width, width)
            block = weight_ref[pl.ds(start + i * size, size), :]
            turned_ref[j, :, i * size : (i + 1) * size] = block.T
    projected_ref[...] = projected


def kept(j):
    return 2 * j + (1 if j else 0)


def split(value, dtype):
    if dtype == F32:
        return [value]
    pieces = []
    for _ in range(PIECES):
        pieces.append(value.astype(dtype))
        value = value - pieces[-1].astype(F32)
    return pieces


def side(count, rows, dtype):
    return LANES * (1 + (1 if dtype == F32 else PIECES) * -(-count // rows))


def put_side(send_ref, start, dots, lines):
    rows, dtype = send_ref.shape[0], send_ref.dtype
    lane = lax.broadcasted_iota(jnp.int32, dots.shape, 1)
    block = jnp.zeros(dots.shape, F32)
    for i, piece in enumerate(split(dots, dtype)):
        block = jnp.where(lane == i, piece.astype(F32), block)
    blocks = [block.astype(dtype)]
    spare = -lines.shape[0] % rows
    if spare:
        lines = jnp.concatenate([lines, jnp.zeros((spare, LANES), F32)], axis=0)
    for piece in split(lines, dtype):
        blocks += [piece[i : i + rows] for i in range(0, piece.shape[0], rows)]
    for i, block in enumerate(blocks):
        send_ref[:, start + i * LANES : start + (i + 1) * LANES] = block


def get_dots(got_ref, start):
    return jnp.sum(got_ref[:, start : start + LANES].astype(F32), axis=1, keepdims=True)


def get_lines(got_ref, start, count):
    rows = got_ref.shape[0]
    each = -(-count // rows)
    blocks = [got_ref[:, i : i + LANES].astype(F32) for i in range(start + LANES, got_ref.shape[1], LANES)]
    total = None
    for i in range(0, len(blocks), each):
        piece = blocks[i] if each == 1 else jnp.concatenate(blocks[i : i + each], axis=0)
        total = piece if total is None else total + piece
    return total[:count]


def products(steps, tp, lhs, weight_ref, out_ref, first=0):
    width = weight_ref.shape[0] // tp
    place = lax.axis_index("tp")
    for j, k in enumerate(steps, first):
        cols = pl.ds(pl.multiple_of((place ^ k) * width, width), width)
        out_ref[:, j * width : (j + 1) * width] = lax.dot_general(
            lhs, weight_ref[cols, :], (((1,), (1,)), ((), ())), preferred_element_type=F32
        )


def row_sum(k, tp, term, rows_ref, gain_ref, inv_rms, dots):
    features = rows_ref.shape[1]
    width = features // tp
    place = lax.axis_index("tp")
    cols = pl.ds(pl.multiple_of((place ^ k) * width, width), width)
    scale = inv_rms * inv_rms * dots * (1.0 / features)
    row = gain_ref[:, cols] * jnp.sum(inv_rms * term, axis=0, keepdims=True)
    return row - jnp.sum(rows_ref[:, cols] * scale, axis=0, keepdims=True)


def sent_kernel(enc, tp, counts_ref, projected_ref, turned_ref, weight_ref, rows_ref, gain_ref, inv_ref, *refs):
    cots = refs[:enc]
    kv_ref, dots_ref, lhs_ref, send_ref, sums_ref = refs[enc:]
    buckets, capacity, columns = kv_ref.shape
    me = lax.axis_index("enc")
    slot = lax.broadcasted_iota(jnp.int32, (capacity, columns), 0)
    blocks = [cot[me].astype(F32) for cot in cots]
    parts = []
    for q in range(buckets):
        block = blocks[0]
        for k in range(1, enc):
            block = jnp.where((me ^ k) == q, blocks[k], block)
        live = slot < counts_ref[:, q : q + 1]
        parts.append(jnp.where(live, block, 0.0))
        kv_ref[q] = jnp.where(live, projected_ref[q * capacity : (q + 1) * capacity, :], 0.0)
    masked = jnp.concatenate(parts, axis=0)
    lhs = masked.astype(BF16)
    lhs_ref[...] = lhs
    steps = [kept(j) ^ 1 for j in range(tp // 2)]
    count, _, width = turned_ref.shape
    for j in range(count):
        send_ref[:, j * width : (j + 1) * width] = jnp.dot(
            lhs, turned_ref[j], preferred_element_type=F32
        )
    products(steps[count:], tp, lhs, weight_ref, send_ref, count)
    dots = jnp.sum(masked * projected_ref[...], axis=1, keepdims=True)
    dots_ref[...] = jnp.broadcast_to(dots, dots_ref.shape)
    width = rows_ref.shape[1] // tp
    chunks, half = width // LANES, tp // 2 * width
    inv_rms = inv_ref[:, :1]
    for j, k in enumerate(steps):
        term = send_ref[:, j * width : (j + 1) * width]
        row = row_sum(k, tp, term, rows_ref, gain_ref, inv_rms, dots)
        for i in range(chunks):
            sums_ref[j * chunks + i : j * chunks + i + 1, :] = row[:, i * LANES : (i + 1) * LANES]
    put_side(send_ref, half, dots_ref[...], sums_ref[...])


def kept_kernel(tp, lhs_ref, weight_ref, rows_ref, gain_ref, inv_ref, dots_ref, kept_ref, sums_ref):
    width = rows_ref.shape[1] // tp
    chunks = width // LANES
    steps = [kept(j) for j in range(tp // 2)]
    products(steps, tp, lhs_ref[...], weight_ref, kept_ref)
    for j, k in enumerate(steps):
        term = kept_ref[:, j * width : (j + 1) * width]
        row = row_sum(k, tp, term, rows_ref, gain_ref, inv_ref[:, :1], dots_ref[:, :1])
        for i in range(chunks):
            sums_ref[j * chunks + i : j * chunks + i + 1, :] = row[:, i * LANES : (i + 1) * LANES]


def fold_kernel(width, got_ref, kept_ref, dots_ref, sums_ref, all_ref, own_ref, *refs):
    pairs = kept_ref.shape[1] // width
    half, chunks = kept_ref.shape[1], width // LANES
    sends, totals = refs[: pairs - 1], refs[pairs - 1 :]
    dots = dots_ref[...] + get_dots(got_ref, half)
    all_ref[...] = dots
    sums = sums_ref[...] + get_lines(got_ref, half, pairs * chunks)
    for j in range(pairs):
        cols = slice(j * width, (j + 1) * width)
        term = kept_ref[:, cols] + got_ref[:, cols]
        lines = sums[j * chunks : (j + 1) * chunks]
        totals[j][...] = lines
        if j:
            for i in range(TERMS):
                piece = term.astype(BF16)
                sends[j - 1][:, i * width : (i + 1) * width] = piece
                term = term - piece.astype(F32)
            put_side(sends[j - 1], TERMS * width, dots, lines)
        else:
            own_ref[...] = term


def pack_kernel(enc, pairs, kv_ref, sum_ref, *refs):
    gots, refs = refs[: pairs - 1], refs[pairs - 1 :]
    sums, (total_ref, *sends) = refs[:-enc], refs[-enc:]
    chunks, capacity = sum_ref.shape[0], kv_ref.shape[1]
    me = lax.axis_index("enc")
    total = sum_ref[...]
    for got in sums:
        total = total + got[...]
    for got in gots:
        start = got.shape[1] - side(chunks, got.shape[0], BF16)
        total = total + get_lines(got, start, chunks)
    total_ref[...] = total
    for k in range(1, enc):
        sends[k - 1][:chunks, :] = total
        block = kv_ref[me ^ k]
        for j in range(block.shape[1] // LANES):
            at = chunks + j * capacity
            sends[k - 1][at : at + capacity, :] = block[:, j * LANES : (j + 1) * LANES]


def combine_kernel(rows_ref, gain_ref, inv_ref, dots_ref, own_ref, *refs):
    gots, (out_ref, token_ref) = refs[:-2], refs[-2:]
    buckets, capacity, width = out_ref.shape
    features = rows_ref.shape[1]
    place = lax.axis_index("tp")
    own = pl.ds(pl.multiple_of(place * width, width), width)
    grad_normed, row_dot = own_ref[...], dots_ref[:, :1]
    for got in gots:
        for i in range(TERMS):
            grad_normed = grad_normed + got[:, i * width : (i + 1) * width].astype(F32)
        row_dot = row_dot + get_dots(got, TERMS * width)
    inv_rms = inv_ref[:, :1]
    first = inv_rms * gain_ref[:, own] * grad_normed
    scale = inv_rms * inv_rms * row_dot * (1.0 / features)
    grad_rows = first - rows_ref[:, own] * scale
    for q in range(buckets):
        out_ref[q] = grad_rows[q * capacity : (q + 1) * capacity].astype(BF16)
    token_ref[...] = jnp.zeros(token_ref.shape, F32)


def final_kernel(enc, total_ref, kv_ref, _, *refs):
    gots, (sum_ref, out_ref) = refs[: enc - 1][::-1], refs[enc - 1 :]
    buckets, capacity, columns = kv_ref.shape
    chunks = total_ref.shape[0]
    me = lax.axis_index("enc")
    total = total_ref[...]
    for got in gots:
        total = total + got[:chunks, :]
    sum_ref[...] = total
    out_ref[me] = kv_ref[me].astype(BF16)
    for k in range(1, enc):
        for j in range(columns // LANES):
            at = chunks + j * capacity
            out_ref[me ^ k, :, j * LANES : (j + 1) * LANES] = gots[k - 1][
                at : at + capacity, :
            ].astype(BF16)


def per_device(visual, counts, merger_bias, norm_gain, kv_weight, kv_cotangent):
    buckets, capacity, features = visual.shape[2:]
    enc, llm, tp = (lax.axis_size(a) for a in ("enc", "llm", "tp"))
    width, columns, rows = features // tp, kv_weight.shape[1], buckets * capacity
    chunks, pairs = width // LANES, tp // 2
    half = pairs * width
    part = functools.partial
    struct = jax.ShapeDtypeStruct
    run = part(call, 2 * kv_weight.size * 2 + 16 * rows * features)

    vis, bias, gain, cot = visual[0, 0], merger_bias[None], norm_gain[None], kv_cotangent[0, 0]
    (token,) = run(
        first_kernel,
        (struct((8, LANES), F32),),
        [pltpu.with_memory_space_constraint(a, pltpu.HBM) for a in (kv_weight, vis, bias, gain)],
        specs=[HBM] * 4,
    )
    projected, inv_rms, turned, inputs = run(
        part(project_kernel, tp),
        (
            struct((rows, columns), F32),
            struct((rows, LANES), F32),
            struct((min(TURNED, pairs), columns, width), BF16),
            struct((rows, features), F32),
        ),
        (vis, bias, gain, kv_weight, token),
        scratch=[pltpu.VMEM((rows, features), BF16)],
    )
    own_cot = cot
    cots = [own_cot] + [swap(cot, "enc", k) for k in range(1, enc)]
    kv, dots, lhs, send = run(
        part(sent_kernel, enc, tp),
        (
            struct((buckets, capacity, columns), F32),
            struct((rows, LANES), F32),
            struct((rows, columns), BF16),
            struct((rows, half + side(pairs * chunks, rows, F32)), F32),
        ),
        (counts[0], projected, turned, kv_weight, inputs, gain, inv_rms, *cots),
        scratch=[pltpu.VMEM((pairs * chunks, LANES), F32)],
    )
    got = swap(send, "tp", 1)
    terms, sums = run(
        part(kept_kernel, tp),
        (struct((rows, half), F32), struct((pairs * chunks, LANES), F32)),
        (lhs, kv_weight, inputs, gain, inv_rms, dots),
    )
    dots, own, *refs = run(
        part(fold_kernel, width),
        (
            struct((rows, LANES), F32),
            struct((rows, width), F32),
            *[struct((rows, TERMS * width + side(chunks, rows, BF16)), BF16)] * (pairs - 1),
            *[struct((chunks, LANES), F32)] * pairs,
        ),
        (got, terms, dots, sums),
    )
    sends, totals = refs[: pairs - 1], refs[pairs - 1 :]
    gots = [swap(s, "tp", kept(j + 1)) for j, s in enumerate(sends)]
    others = [
        swap(t, ("llm", "tp"), tp * g + kept(j)) for g in range(1, llm) for j, t in enumerate(totals)
    ]
    total, *sends = run(
        part(pack_kernel, enc, pairs),
        (
            struct((chunks, LANES), F32),
            *[struct((chunks + capacity * columns // LANES, LANES), F32)] * (enc - 1),
        ),
        (kv, totals[0], *gots, *others[::-1]),
    )
    visual_grad, token = run(
        combine_kernel,
        (struct((buckets, capacity, width), BF16), struct((8, LANES), F32)),
        (inputs, gain, inv_rms, dots, own, *gots),
    )
    gots = [swap(s, "enc", k + 1) for k, s in enumerate(sends)]
    bias_grad, key_values = run(
        part(final_kernel, enc),
        (struct((chunks, LANES), F32), struct((buckets, capacity, columns), BF16)),
        (total, kv, token, *gots[::-1]),
    )
    return (key_values[None, None], visual_grad[None, None], bias_grad.reshape(width))


def solution(mesh):
    return jax.shard_map(
        per_device,
        mesh=mesh,
        in_specs=(
            P("enc", "llm", None, None, None),
            P("enc", "llm", None),
            P(),
            P(),
            P(None, "tp"),
            P("enc", "llm", None, None, "tp"),
        ),
        out_specs=(P("enc", "llm", None, None, "tp"), P("enc", "llm", None, None, "tp"), P("tp")),
        check_vma=False,
    )
```

```python
import functools

import jax
import jax.numpy as jnp
from jax import lax
from jax.experimental import pallas as pl
from jax.experimental.pallas import tpu as pltpu
from jax.sharding import PartitionSpec as P

LANES = 128
PIECES = 3
TERMS = 2
STEPS = 8
TURNED = 2
VMEM = pl.BlockSpec(memory_space=pltpu.VMEM)
HBM = pl.BlockSpec(memory_space=pltpu.HBM)
F32 = jnp.float32
BF16 = jnp.bfloat16


def swap(x, axis, k):
    n = lax.axis_size(axis)
    return lax.ppermute(x, axis, [(i, i ^ k) for i in range(n)])


def call(limit, kernel, outs, args, scratch=(), specs=None):
    return pl.pallas_call(
        kernel,
        out_shape=tuple(outs),
        in_specs=specs or [VMEM] * len(args),
        out_specs=tuple(VMEM for _ in outs),
        scratch_shapes=list(scratch),
        compiler_params=pltpu.CompilerParams(vmem_limit_bytes=limit),
    )(*args)


def first_kernel(*refs):
    token_ref = refs[-1]
    token_ref[...] = jnp.zeros(token_ref.shape, F32)


def project_kernel(
    tp, vis_ref, bias_ref, gain_ref, weight_ref, _, projected_ref, inv_ref, turned_ref, rows_ref, normed_ref
):
    buckets, capacity, features = vis_ref.shape
    for q in range(buckets):
        rows_ref[q * capacity : (q + 1) * capacity, :] = vis_ref[q].astype(F32) + bias_ref[...]
    inputs = rows_ref[...]
    mean = jnp.sum(inputs * inputs, axis=1, keepdims=True) / features
    inv_rms = lax.rsqrt(mean + 1e-06)
    normed_ref[...] = (inputs * inv_rms * gain_ref[...]).astype(BF16)
    inv_ref[...] = jnp.broadcast_to(inv_rms, inv_ref.shape)
    count, width = turned_ref.shape[0], features // tp
    place, step = lax.axis_index("tp"), features // STEPS
    projected = jnp.zeros(projected_ref.shape, F32)
    for i in range(STEPS):
        part = slice(i * step, (i + 1) * step)
        projected = projected + jnp.dot(
            normed_ref[:, part], weight_ref[part, :], preferred_element_type=F32
        )
        size = width // STEPS
        for j in range(count):
            start = pl.multiple_of((place ^ kept(j) ^ 1) * width, width)
            block = weight_ref[pl.ds(start + i * size, size), :]
            turned_ref[j, :, i * size : (i + 1) * size] = block.T
    projected_ref[...] = projected


def kept(j):
    return 2 * j + (1 if j else 0)


def split(value, dtype):
    if dtype == F32:
        return [value]
    pieces = []
    for _ in range(PIECES):
        pieces.append(value.astype(dtype))
        value = value - pieces[-1].astype(F32)
    return pieces


def side(count, rows, dtype):
    return LANES * (1 + (1 if dtype == F32 else PIECES) * -(-count // rows))


def put_side(send_ref, start, dots, lines):
    rows, dtype = send_ref.shape[0], send_ref.dtype
    lane = lax.broadcasted_iota(jnp.int32, dots.shape, 1)
    block = jnp.zeros(dots.shape, F32)
    for i, piece in enumerate(split(dots, dtype)):
        block = jnp.where(lane == i, piece.astype(F32), block)
    blocks = [block.astype(dtype)]
    spare = -lines.shape[0] % rows
    if spare:
        lines = jnp.concatenate([lines, jnp.zeros((spare, LANES), F32)], axis=0)
    for piece in split(lines, dtype):
        blocks += [piece[i : i + rows] for i in range(0, piece.shape[0], rows)]
    for i, block in enumerate(blocks):
        send_ref[:, start + i * LANES : start + (i + 1) * LANES] = block


def get_dots(got_ref, start):
    return jnp.sum(got_ref[:, start : start + LANES].astype(F32), axis=1, keepdims=True)


def get_lines(got_ref, start, count):
    rows = got_ref.shape[0]
    each = -(-count // rows)
    blocks = [got_ref[:, i : i + LANES].astype(F32) for i in range(start + LANES, got_ref.shape[1], LANES)]
    total = None
    for i in range(0, len(blocks), each):
        piece = blocks[i] if each == 1 else jnp.concatenate(blocks[i : i + each], axis=0)
        total = piece if total is None else total + piece
    return total[:count]


def products(steps, tp, lhs, weight_ref, out_ref, first=0):
    width = weight_ref.shape[0] // tp
    place = lax.axis_index("tp")
    for j, k in enumerate(steps, first):
        cols = pl.ds(pl.multiple_of((place ^ k) * width, width), width)
        out_ref[:, j * width : (j + 1) * width] = lax.dot_general(
            lhs, weight_ref[cols, :], (((1,), (1,)), ((), ())), preferred_element_type=F32
        )


def row_sum(k, tp, term, rows_ref, gain_ref, inv_rms, dots):
    features = rows_ref.shape[1]
    width = features // tp
    place = lax.axis_index("tp")
    cols = pl.ds(pl.multiple_of((place ^ k) * width, width), width)
    scale = inv_rms * inv_rms * dots * (1.0 / features)
    row = gain_ref[:, cols] * jnp.sum(inv_rms * term, axis=0, keepdims=True)
    return row - jnp.sum(rows_ref[:, cols] * scale, axis=0, keepdims=True)


def sent_kernel(enc, tp, counts_ref, projected_ref, turned_ref, weight_ref, rows_ref, gain_ref, inv_ref, *refs):
    cots = refs[:enc]
    dots_ref, lhs_ref, send_ref, sums_ref = refs[enc:]
    buckets, capacity, columns = cots[0].shape
    me = lax.axis_index("enc")
    slot = lax.broadcasted_iota(jnp.int32, (capacity, columns), 0)
    blocks = [cot[me].astype(F32) for cot in cots]
    parts = []
    for q in range(buckets):
        block = blocks[0]
        for k in range(1, enc):
            block = jnp.where((me ^ k) == q, blocks[k], block)
        live = slot < counts_ref[:, q : q + 1]
        parts.append(jnp.where(live, block, 0.0))
    masked = jnp.concatenate(parts, axis=0)
    lhs = masked.astype(BF16)
    lhs_ref[...] = lhs
    steps = [kept(j) ^ 1 for j in range(tp // 2)]
    count, _, width = turned_ref.shape
    for j in range(count):
        send_ref[:, j * width : (j + 1) * width] = jnp.dot(
            lhs, turned_ref[j], preferred_element_type=F32
        )
    products(steps[count:], tp, lhs, weight_ref, send_ref, count)
    dots = jnp.sum(masked * projected_ref[...], axis=1, keepdims=True)
    dots_ref[...] = jnp.broadcast_to(dots, dots_ref.shape)
    width = rows_ref.shape[1] // tp
    chunks, half = width // LANES, tp // 2 * width
    inv_rms = inv_ref[:, :1]
    for j, k in enumerate(steps):
        term = send_ref[:, j * width : (j + 1) * width]
        row = row_sum(k, tp, term, rows_ref, gain_ref, inv_rms, dots)
        for i in range(chunks):
            sums_ref[j * chunks + i : j * chunks + i + 1, :] = row[:, i * LANES : (i + 1) * LANES]
    put_side(send_ref, half, dots_ref[...], sums_ref[...])


def kept_kernel(tp, counts_ref, projected_ref, lhs_ref, weight_ref, rows_ref, gain_ref, inv_ref, dots_ref, kept_ref, sums_ref, kv_ref):
    width = rows_ref.shape[1] // tp
    chunks = width // LANES
    steps = [kept(j) for j in range(tp // 2)]
    products(steps, tp, lhs_ref[...], weight_ref, kept_ref)
    for j, k in enumerate(steps):
        term = kept_ref[:, j * width : (j + 1) * width]
        row = row_sum(k, tp, term, rows_ref, gain_ref, inv_ref[:, :1], dots_ref[:, :1])
        for i in range(chunks):
            sums_ref[j * chunks + i : j * chunks + i + 1, :] = row[:, i * LANES : (i + 1) * LANES]
    buckets, capacity, columns = kv_ref.shape
    slot = lax.broadcasted_iota(jnp.int32, (capacity, columns), 0)
    for q in range(buckets):
        part = projected_ref[q * capacity : (q + 1) * capacity, :]
        kv_ref[q] = jnp.where(slot < counts_ref[:, q : q + 1], part, 0.0)


def fold_kernel(width, got_ref, kept_ref, dots_ref, sums_ref, all_ref, own_ref, *refs):
    pairs = kept_ref.shape[1] // width
    half, chunks = kept_ref.shape[1], width // LANES
    sends, totals = refs[: pairs - 1], refs[pairs - 1 :]
    dots = dots_ref[...] + get_dots(got_ref, half)
    all_ref[...] = dots
    sums = sums_ref[...] + get_lines(got_ref, half, pairs * chunks)
    for j in range(pairs):
        cols = slice(j * width, (j + 1) * width)
        term = kept_ref[:, cols] + got_ref[:, cols]
        lines = sums[j * chunks : (j + 1) * chunks]
        totals[j][...] = lines
        if j:
            for i in range(TERMS):
                piece = term.astype(BF16)
                sends[j - 1][:, i * width : (i + 1) * width] = piece
                term = term - piece.astype(F32)
            put_side(sends[j - 1], TERMS * width, dots, lines)
        else:
            own_ref[...] = term


def pack_kernel(enc, pairs, kv_ref, sum_ref, *refs):
    gots, refs = refs[: pairs - 1], refs[pairs - 1 :]
    sums, (total_ref, *sends) = refs[:-enc], refs[-enc:]
    chunks, capacity = sum_ref.shape[0], kv_ref.shape[1]
    me = lax.axis_index("enc")
    total = sum_ref[...]
    for got in sums:
        total = total + got[...]
    for got in gots:
        start = got.shape[1] - side(chunks, got.shape[0], BF16)
        total = total + get_lines(got, start, chunks)
    total_ref[...] = total
    for k in range(1, enc):
        sends[k - 1][:chunks, :] = total
        block = kv_ref[me ^ k]
        for j in range(block.shape[1] // LANES):
            at = chunks + j * capacity
            sends[k - 1][at : at + capacity, :] = block[:, j * LANES : (j + 1) * LANES]


def combine_kernel(rows_ref, gain_ref, inv_ref, dots_ref, own_ref, *refs):
    gots, (out_ref, token_ref) = refs[:-2], refs[-2:]
    buckets, capacity, width = out_ref.shape
    features = rows_ref.shape[1]
    place = lax.axis_index("tp")
    own = pl.ds(pl.multiple_of(place * width, width), width)
    grad_normed, row_dot = own_ref[...], dots_ref[:, :1]
    for got in gots:
        for i in range(TERMS):
            grad_normed = grad_normed + got[:, i * width : (i + 1) * width].astype(F32)
        row_dot = row_dot + get_dots(got, TERMS * width)
    inv_rms = inv_ref[:, :1]
    first = inv_rms * gain_ref[:, own] * grad_normed
    scale = inv_rms * inv_rms * row_dot * (1.0 / features)
    grad_rows = first - rows_ref[:, own] * scale
    for q in range(buckets):
        out_ref[q] = grad_rows[q * capacity : (q + 1) * capacity].astype(BF16)
    token_ref[...] = jnp.zeros(token_ref.shape, F32)


def final_kernel(enc, total_ref, kv_ref, _, *refs):
    gots, (sum_ref, out_ref) = refs[: enc - 1][::-1], refs[enc - 1 :]
    buckets, capacity, columns = kv_ref.shape
    chunks = total_ref.shape[0]
    me = lax.axis_index("enc")
    total = total_ref[...]
    for got in gots:
        total = total + got[:chunks, :]
    sum_ref[...] = total
    out_ref[me] = kv_ref[me].astype(BF16)
    for k in range(1, enc):
        for j in range(columns // LANES):
            at = chunks + j * capacity
            out_ref[me ^ k, :, j * LANES : (j + 1) * LANES] = gots[k - 1][
                at : at + capacity, :
            ].astype(BF16)


def per_device(visual, counts, merger_bias, norm_gain, kv_weight, kv_cotangent):
    buckets, capacity, features = visual.shape[2:]
    enc, llm, tp = (lax.axis_size(a) for a in ("enc", "llm", "tp"))
    width, columns, rows = features // tp, kv_weight.shape[1], buckets * capacity
    chunks, pairs = width // LANES, tp // 2
    half = pairs * width
    part = functools.partial
    struct = jax.ShapeDtypeStruct
    run = part(call, 2 * kv_weight.size * 2 + 16 * rows * features)

    vis, bias, gain, cot = visual[0, 0], merger_bias[None], norm_gain[None], kv_cotangent[0, 0]
    (token,) = run(
        first_kernel,
        (struct((8, LANES), F32),),
        [pltpu.with_memory_space_constraint(a, pltpu.HBM) for a in (kv_weight, vis, bias, gain)],
        specs=[HBM] * 4,
    )
    projected, inv_rms, turned, inputs = run(
        part(project_kernel, tp),
        (
            struct((rows, columns), F32),
            struct((rows, LANES), F32),
            struct((min(TURNED, pairs), columns, width), BF16),
            struct((rows, features), F32),
        ),
        (vis, bias, gain, kv_weight, token),
        scratch=[pltpu.VMEM((rows, features), BF16)],
    )
    own_cot = cot
    cots = [own_cot] + [swap(cot, "enc", k) for k in range(1, enc)]
    dots, lhs, send = run(
        part(sent_kernel, enc, tp),
        (
            struct((rows, LANES), F32),
            struct((rows, columns), BF16),
            struct((rows, half + side(pairs * chunks, rows, F32)), F32),
        ),
        (counts[0], projected, turned, kv_weight, inputs, gain, inv_rms, *cots),
        scratch=[pltpu.VMEM((pairs * chunks, LANES), F32)],
    )
    got = swap(send, "tp", 1)
    terms, sums, kv = run(
        part(kept_kernel, tp),
        (
            struct((rows, half), F32),
            struct((pairs * chunks, LANES), F32),
            struct((buckets, capacity, columns), F32),
        ),
        (counts[0], projected, lhs, kv_weight, inputs, gain, inv_rms, dots),
    )
    dots, own, *refs = run(
        part(fold_kernel, width),
        (
            struct((rows, LANES), F32),
            struct((rows, width), F32),
            *[struct((rows, TERMS * width + side(chunks, rows, BF16)), BF16)] * (pairs - 1),
            *[struct((chunks, LANES), F32)] * pairs,
        ),
        (got, terms, dots, sums),
    )
    sends, totals = refs[: pairs - 1], refs[pairs - 1 :]
    gots = [swap(s, "tp", kept(j + 1)) for j, s in enumerate(sends)]
    others = [
        swap(t, ("llm", "tp"), tp * g + kept(j)) for g in range(1, llm) for j, t in enumerate(totals)
    ]
    total, *sends = run(
        part(pack_kernel, enc, pairs),
        (
            struct((chunks, LANES), F32),
            *[struct((chunks + capacity * columns // LANES, LANES), F32)] * (enc - 1),
        ),
        (kv, totals[0], *gots, *others[::-1]),
    )
    visual_grad, token = run(
        combine_kernel,
        (struct((buckets, capacity, width), BF16), struct((8, LANES), F32)),
        (inputs, gain, inv_rms, dots, own, *gots),
    )
    gots = [swap(s, "enc", k + 1) for k, s in enumerate(sends)]
    bias_grad, key_values = run(
        part(final_kernel, enc),
        (struct((chunks, LANES), F32), struct((buckets, capacity, columns), BF16)),
        (total, kv, token, *gots[::-1]),
    )
    return (key_values[None, None], visual_grad[None, None], bias_grad.reshape(width))


def solution(mesh):
    return jax.shard_map(
        per_device,
        mesh=mesh,
        in_specs=(
            P("enc", "llm", None, None, None),
            P("enc", "llm", None),
            P(),
            P(),
            P(None, "tp"),
            P("enc", "llm", None, None, "tp"),
        ),
        out_specs=(P("enc", "llm", None, None, "tp"), P("enc", "llm", None, None, "tp"), P("tp")),
        check_vma=False,
    )
```
